256 devices in a mesh: lat: 8 (over x, y_hi), lon: 32 (over y_lo, z, core).
Axes of the slice: x: 4, y: 4 (y_hi: 2, y_lo: 2; y = y_hi * 2 + y_lo), z: 8, core: 2. Of those that a mesh axis runs over, the one named last changes fastest.
Arguments:
- field: float32 [160, 640, 384], P('lat', 'lon'), may hold values from -6 to 6
- lat_kernel: float32 [41], replicated, may hold values from 0.0121951215 to 0.036585364
- lon_kernel: float32 [41], replicated, may hold values from 0.0121951215 to 0.036585364
- time_taps: float32 [129], replicated, may hold values from -0.0058139535 to 0.0058139535
Outputs:
- basis: float32 [160, 640, 256], P('lat', 'lon')
- merged_factor: float32 [256, 256], replicated
The draws below stay inside these ranges and needn't reach their ends.
All inputs are finite; a program needn't handle non-finite values.
Results may differ from the reference program's by a relative error of at most 0.00016.
Values sent between devices are 32-bit elements; how exact they have to be, the bound alone decides.
No kernel may reach another device: no remote copies, remote signals or barrier semaphores. Data moves between devices by JAX's collectives and lax.ppermute only.
A program may use at most 64 MiB of HBM per device.

```python
import jax
import jax.numpy as jnp
from jax import lax

TH = 64
SH = 20
TIN = 384
NLAT = 160
NLON = 640


def block_levels(rng, shape, pieces, smallest, top_value):
    level = 1.0
    for axis_at, shards_of in pieces:
        steps = jax.random.uniform(jax.random.fold_in(jax.random.fold_in(rng, 6), axis_at), (shards_of,), jnp.float32, smallest / len(pieces), top_value / len(pieces))
        level = level * jnp.repeat(jnp.exp(steps), shape[axis_at] // shards_of).reshape((-1,) + (1,) * (len(shape) - 1 - axis_at))
    return level


def normal_values(own_key, shape, spread, limit, cuts=(), kind=jnp.bfloat16):
    result = jax.random.normal(own_key, shape, jnp.float32) * spread
    if len(cuts) > 0:
        result = block_levels(own_key, shape, cuts, -0.22, 0.18) * result
    return jnp.clip(result, min=-limit, max=limit).astype(kind)


def setup_inputs(seed: int = 0) -> dict:
    arg_keys = jax.random.split(jax.random.key(seed), 5)
    return {
        "field": normal_values(arg_keys[0], (NLAT, NLON, TIN), 1.0, 6.0, ((0, 8), (1, 32)), jnp.float32),
        "lat_kernel": jnp.clip(jax.random.uniform(arg_keys[1], (2 * SH + 1,), jnp.float32, 0.0121951215, 0.036585364), 0.0121951215, 0.036585364),
        "lon_kernel": jnp.clip(jax.random.uniform(arg_keys[2], (2 * SH + 1,), jnp.float32, 0.0121951215, 0.036585364), 0.0121951215, 0.036585364),
        "time_taps": jnp.clip(jax.random.uniform(arg_keys[3], (2 * TH + 1,), jnp.float32, -0.0058139535, 0.0058139535), -0.0058139535, 0.0058139535),
    }


def reference(field, lat_kernel, lon_kernel, time_taps):
    nrows, ncols, length_in = field.shape
    steps_out = length_in - 2 * TH
    source = lax.broadcasted_iota(jnp.int32, (length_in, steps_out), 0)
    target = lax.broadcasted_iota(jnp.int32, (length_in, steps_out), 1)
    offset = source - target
    inside = (offset >= 0) & (offset <= 2 * TH)
    toeplitz = jnp.where(inside, time_taps[jnp.clip(offset, 0, 2 * TH)], jnp.float32(0.0))
    toeplitz = toeplitz + jnp.where(offset == TH, jnp.float32(1.0), jnp.float32(0.0))
    filtered = jnp.dot(field.reshape(-1, length_in).astype(jnp.float32), toeplitz.astype(jnp.float32), precision=lax.Precision.HIGHEST, preferred_element_type=jnp.float32).reshape(nrows, ncols, steps_out)
    padded = jnp.pad(filtered, ((SH, SH), (0, 0), (0, 0)))
    lat_done = jnp.zeros_like(filtered)
    for shift_k in range(2 * SH + 1):
        lat_done = lat_done + lat_kernel[shift_k] * padded[shift_k:shift_k + nrows]
    wrapped = jnp.concatenate([lat_done[:, ncols - SH:], lat_done, lat_done[:, :SH]], axis=1)
    smooth = jnp.zeros_like(filtered)
    for shift_k in range(2 * SH + 1):
        smooth = smooth + lon_kernel[shift_k] * wrapped[:, shift_k:shift_k + ncols]
    latitude = jnp.pi * (jnp.arange(nrows, dtype=jnp.float32) + 0.5) / nrows - jnp.pi / 2
    weights = jnp.sqrt(jnp.cos(latitude))
    matrix = (smooth * weights[:, None, None]).reshape(-1, steps_out)
    gram = lax.dot_general(matrix.astype(jnp.float32), matrix.astype(jnp.float32), (((0,), (0,)), ((), ())), precision=lax.Precision.HIGHEST, preferred_element_type=jnp.float32)
    lower = jnp.linalg.cholesky(gram)
    scale = jnp.sqrt(jnp.float32(nrows * ncols))
    solved = lax.linalg.triangular_solve(lower, matrix, left_side=False, lower=True, transpose_a=True)
    basis = (solved * scale).reshape(nrows, ncols, steps_out)
    return (basis, lower.T / scale)
```

```python
import jax
import jax.numpy as jnp
from jax import lax
from jax.sharding import PartitionSpec as P

TH = 64
SH = 20
LAT = ("x", "yh")
LON = ("yl", "z", "core")


def extended_2(value, sides, width, wrap):
    for axis, dim in sides:
        peers, length = (lax.axis_size(axis), value.shape[dim])
        up = [(i, (i + 1) % peers) for i in range(peers if wrap else peers - 1)]
        down = [(j, i) for i, j in up]
        last = lax.slice_in_dim(value, length - width, length, axis=dim)
        initial = lax.slice_in_dim(value, 0, width, axis=dim)
        before = lax.ppermute(last, axis, up)
        after = lax.ppermute(initial, axis, down)
        value = jnp.concatenate([before, value, after], axis=dim)
    return value


def skewed(coeffs, count, width):
    period = jnp.pad(coeffs, (0, count))
    flat = jnp.tile(period, count)[: count * width]
    return flat.reshape(count, width)


def banded(kernel, count):
    return skewed(kernel, count, count + 2 * SH)


def smooth_rows(band, extended):
    rows_in, cols_in, hours = extended.shape
    flat = extended.reshape(rows_in, cols_in * hours)
    result = jnp.dot(
        band, flat, precision=lax.Precision.HIGHEST, preferred_element_type=jnp.float32
    )
    return result.reshape(band.shape[0], cols_in, hours)


PLANE = ("x", "yh", "yl")


def shared(value, axes):
    peers = lax.axis_size(axes)
    copies = jnp.broadcast_to(value[None], (peers,) + value.shape)
    return lax.all_to_all(copies, axes, 0, 0)


def summed(value):
    swap = [(0, 1), (1, 0)]
    core = lax.axis_index("core")
    rows, cols = value.shape
    half = rows // 2
    kept = lax.dynamic_slice_in_dim(value, core * half, half, 0)
    given = lax.dynamic_slice_in_dim(value, (1 - core) * half, half, 0)
    kept = kept + lax.ppermute(given, "core", swap)
    peers = lax.axis_size(PLANE)
    pieces = lax.all_to_all(kept.reshape(peers, half // peers, cols), PLANE, 0, 0)
    piece = shared(pieces.sum(axis=0), ("z",)).sum(axis=0)
    kept = shared(piece, PLANE).reshape(half, cols)
    given = lax.ppermute(kept, "core", swap)
    top = jnp.where(core == 0, kept, given)
    bottom = jnp.where(core == 0, given, kept)
    return jnp.concatenate([top, bottom], axis=0)


def body(field, lat_kernel, lon_kernel, time_taps):
    rows_lat, rows_lon, length_in = field.shape
    steps_out = length_in - 2 * TH
    lat_place = lax.axis_index(LAT)
    total_lat = rows_lat * lax.axis_size(LAT)
    cells = total_lat * rows_lon * lax.axis_size(LON)
    centre = (jnp.arange(2 * TH + 1, dtype=jnp.int32) == TH).astype(jnp.float32)
    taps_full = time_taps + centre
    skew_time = skewed(taps_full, steps_out, length_in)
    filtered = lax.dot_general(
        field.reshape(-1, length_in),
        skew_time,
        (((1,), (1,)), ((), ())),
        precision=lax.Precision.HIGHEST,
        preferred_element_type=jnp.float32,
    ).reshape(rows_lat, rows_lon, steps_out)
    lat_band = banded(lat_kernel, rows_lat)
    lon_band = banded(lon_kernel, rows_lon)
    extended = extended_2(filtered, ((LAT, 0),), SH, False)
    narrow = smooth_rows(lat_band, extended)
    lat_done = extended_2(narrow, ((LON, 1),), SH, True)
    smooth = jnp.einsum(
        "jk,ikt->ijt",
        lon_band,
        lat_done,
        precision=lax.Precision.HIGHEST,
        preferred_element_type=jnp.float32,
    )
    globrow = (lat_place * rows_lat + jnp.arange(rows_lat, dtype=jnp.int32)).astype(jnp.float32)
    latitude = jnp.pi * (globrow + 0.5) / total_lat - jnp.pi / 2
    weights = jnp.sqrt(jnp.cos(latitude))
    matrix = (smooth * weights[:, None, None]).reshape(-1, steps_out)
    local_gram = lax.dot_general(
        matrix,
        matrix,
        (((0,), (0,)), ((), ())),
        precision=lax.Precision.HIGHEST,
        preferred_element_type=jnp.float32,
    )
    gram = summed(local_gram)
    lower = jnp.linalg.cholesky(gram)
    scale = jnp.sqrt(jnp.float32(cells))
    identity = jnp.eye(steps_out, dtype=jnp.float32)
    inverse = lax.linalg.triangular_solve(lower, identity, left_side=True, lower=True)
    solved = lax.dot_general(
        matrix,
        inverse,
        (((1,), (1,)), ((), ())),
        precision=lax.Precision.HIGHEST,
        preferred_element_type=jnp.float32,
    )
    basis = (solved * scale).reshape(rows_lat, rows_lon, steps_out)
    return (basis, lower.T / scale)


def solution(mesh):
    fine = jax.sharding.Mesh(mesh.devices.reshape(4, 2, 2, 8, 2), ("x", "yh", "yl", "z", "core"))
    placed = (P(LAT, LON, None), P(), P(), P())
    return jax.shard_map(
        body, mesh=fine, in_specs=placed, out_specs=(P(LAT, LON, None), P()), check_vma=False
    )
```

```python
import functools

import jax
import jax.numpy as jnp
from jax import lax
from jax.experimental import pallas as pl
from jax.experimental.pallas import tpu as pltpu
from jax.sharding import PartitionSpec as P

TH = 64
SH = 20
LAT = ("x", "yh")
LON = ("yl", "z", "core")


def extended_2(value, sides, width, wrap):
    for axis, dim in sides:
        peers, length = (lax.axis_size(axis), value.shape[dim])
        up = [(i, (i + 1) % peers) for i in range(peers if wrap else peers - 1)]
        down = [(j, i) for i, j in up]
        last = lax.slice_in_dim(value, length - width, length, axis=dim)
        initial = lax.slice_in_dim(value, 0, width, axis=dim)
        before = lax.ppermute(last, axis, up)
        after = lax.ppermute(initial, axis, down)
        value = jnp.concatenate([before, value, after], axis=dim)
    return value


def skewed(coeffs, count, width):
    period = jnp.pad(coeffs, (0, count))
    flat = jnp.tile(period, count)[: count * width]
    return flat.reshape(count, width)


def banded(kernel, count):
    return skewed(kernel, count, count + 2 * SH)


def smooth_rows(band, extended):
    rows_in, cols_in, hours = extended.shape
    flat = extended.reshape(rows_in, cols_in * hours)
    result = jnp.dot(
        band, flat, precision=lax.Precision.HIGHEST, preferred_element_type=jnp.float32
    )
    return result.reshape(band.shape[0], cols_in, hours)


PLANE = ("x", "yh", "yl")


def shared(value, axes):
    peers = lax.axis_size(axes)
    copies = jnp.broadcast_to(value[None], (peers,) + value.shape)
    return lax.all_to_all(copies, axes, 0, 0)


def summed(value):
    swap = [(0, 1), (1, 0)]
    core = lax.axis_index("core")
    rows, cols = value.shape
    half = rows // 2
    kept = lax.dynamic_slice_in_dim(value, core * half, half, 0)
    given = lax.dynamic_slice_in_dim(value, (1 - core) * half, half, 0)
    kept = kept + lax.ppermute(given, "core", swap)
    peers = lax.axis_size(PLANE)
    pieces = lax.all_to_all(kept.reshape(peers, half // peers, cols), PLANE, 0, 0)
    piece = shared(pieces.sum(axis=0), ("z",)).sum(axis=0)
    kept = shared(piece, PLANE).reshape(half, cols)
    given = lax.ppermute(kept, "core", swap)
    top = jnp.where(core == 0, kept, given)
    bottom = jnp.where(core == 0, given, kept)
    return jnp.concatenate([top, bottom], axis=0)


TILE = 128
STEP = 8

def product(left, right, over):
    return lax.dot_general(
        left,
        right,
        (over, ((), ())),
        precision=lax.Precision.HIGHEST,
        preferred_element_type=jnp.float32,
    )


def wide(value):
    return jnp.broadcast_to(value, (STEP, TILE))


def eliminate(work):
    for top in range(0, TILE, STEP):
        own = work[top:top + STEP, :TILE]
        cols = [wide(own[:, top + j:top + j + 1]) for j in range(STEP)]
        left = {(i, j): wide(cols[j][i:i + 1, :]) for j in range(STEP) for i in range(j + 1)}
        rows = [[wide(work[top + i:top + i + 1, s:s + TILE]) for s in (0, TILE)] for i in range(STEP)]
        root, upper = [], {}
        for j in range(STEP):
            root.append(lax.rsqrt(left[j, j]))
            for i in range(j + 1, STEP):
                upper[j, i] = left[j, i] * root[j]
            for i in range(j + 1, STEP):
                for n in range(i, STEP):
                    left[i, n] = left[i, n] - upper[j, i] * upper[j, n]
        for j in range(STEP):
            rows[j] = [value * root[j] for value in rows[j]]
            for i in range(j + 1, STEP):
                rows[i] = [value - upper[j, i] * done for value, done in zip(rows[i], rows[j])]
        for j in range(STEP):
            for half in range(2):
                work[top + j:top + j + 1, half * TILE:(half + 1) * TILE] = rows[j][half][:1, :]
        for below in range(top + STEP, TILE, STEP):
            parts = [work[below:below + STEP, s:s + TILE] for s in (0, TILE)]
            factors = [wide(parts[0][:, top + j:top + j + 1]) for j in range(STEP)]
            for j in range(STEP):
                factors[j] = factors[j] * root[j]
                for i in range(j + 1, STEP):
                    factors[i] = factors[i] - upper[j, i] * factors[j]
            for j in range(STEP):
                parts = [value - factors[j] * done for value, done in zip(parts, rows[j])]
            for half in range(2):
                work[below:below + STEP, half * TILE:(half + 1) * TILE] = parts[half]


ROWS = ((0,), (0,))
COLS = ((1,), (1,))
PLAIN = ((1,), (0,))


def factor_kernel(cells, gram, matrix, basis, merged, work):
    row = lax.broadcasted_iota(jnp.int32, (TILE, TILE), 0)
    col = lax.broadcasted_iota(jnp.int32, (TILE, TILE), 1)
    eye = jnp.where(row == col, 1.0, 0.0).astype(jnp.float32)
    scale = float(cells) ** 0.5

    def solve(block):
        work[:, :TILE] = block
        work[:, TILE:] = eye
        eliminate(work)
        upper = jnp.where(row <= col, work[:, :TILE], 0.0)
        lower = jnp.where(row >= col, work[:, TILE:], 0.0)
        return upper, lower

    r11, w11 = solve(gram[:TILE, :TILE])
    r12 = product(w11, gram[:TILE, TILE:], PLAIN)
    r22, w22 = solve(gram[TILE:, TILE:] - product(r12, r12, ROWS))
    w21 = -product(w22, product(r12, w11, ROWS), PLAIN)
    merged[:TILE, :TILE] = r11 * (1.0 / scale)
    merged[:TILE, TILE:] = r12 * (1.0 / scale)
    merged[TILE:, :TILE] = jnp.zeros((TILE, TILE), jnp.float32)
    merged[TILE:, TILE:] = r22 * (1.0 / scale)
    first, second = (matrix[:, :TILE], matrix[:, TILE:])
    basis[:, :TILE] = product(first, w11 * scale, COLS)
    basis[:, TILE:] = product(first, w21 * scale, COLS) + product(second, w22 * scale, COLS)


def factored(gram, matrix, cells):
    like = jax.ShapeDtypeStruct
    return pl.pallas_call(
        functools.partial(factor_kernel, cells),
        out_shape=(like(matrix.shape, jnp.float32), like(gram.shape, jnp.float32)),
        scratch_shapes=[pltpu.VMEM((TILE, 2 * TILE), jnp.float32)],
        compiler_params=pltpu.CompilerParams(vmem_limit_bytes=32 * 1024 * 1024),
        name="factor",
    )(gram, matrix)


def body(field, lat_kernel, lon_kernel, time_taps):
    rows_lat, rows_lon, length_in = field.shape
    steps_out = length_in - 2 * TH
    lat_place = lax.axis_index(LAT)
    total_lat = rows_lat * lax.axis_size(LAT)
    cells = total_lat * rows_lon * lax.axis_size(LON)
    centre = (jnp.arange(2 * TH + 1, dtype=jnp.int32) == TH).astype(jnp.float32)
    taps_full = time_taps + centre
    skew_time = skewed(taps_full, steps_out, length_in)
    filtered = lax.dot_general(
        field.reshape(-1, length_in),
        skew_time,
        (((1,), (1,)), ((), ())),
        precision=lax.Precision.HIGHEST,
        preferred_element_type=jnp.float32,
    ).reshape(rows_lat, rows_lon, steps_out)
    lat_band = banded(lat_kernel, rows_lat)
    lon_band = banded(lon_kernel, rows_lon)
    extended = extended_2(filtered, ((LAT, 0),), SH, False)
    narrow = smooth_rows(lat_band, extended)
    lat_done = extended_2(narrow, ((LON, 1),), SH, True)
    smooth = jnp.einsum(
        "jk,ikt->ijt",
        lon_band,
        lat_done,
        precision=lax.Precision.HIGHEST,
        preferred_element_type=jnp.float32,
    )
    globrow = (lat_place * rows_lat + jnp.arange(rows_lat, dtype=jnp.int32)).astype(jnp.float32)
    latitude = jnp.pi * (globrow + 0.5) / total_lat - jnp.pi / 2
    weights = jnp.sqrt(jnp.cos(latitude))
    matrix = (smooth * weights[:, None, None]).reshape(-1, steps_out)
    local_gram = lax.dot_general(
        matrix,
        matrix,
        (((0,), (0,)), ((), ())),
        precision=lax.Precision.HIGHEST,
        preferred_element_type=jnp.float32,
    )
    gram = summed(local_gram)
    basis, merged = factored(gram, matrix, cells)
    return (basis.reshape(rows_lat, rows_lon, steps_out), merged)


def solution(mesh):
    fine = jax.sharding.Mesh(mesh.devices.reshape(4, 2, 2, 8, 2), ("x", "yh", "yl", "z", "core"))
    placed = (P(LAT, LON, None), P(), P(), P())
    return jax.shard_map(
        body, mesh=fine, in_specs=placed, out_specs=(P(LAT, LON, None), P()), check_vma=False
    )
```

```python
import functools

import jax
import jax.numpy as jnp
from jax import lax
from jax.experimental import pallas as pl
from jax.experimental.pallas import tpu as pltpu
from jax.sharding import PartitionSpec as P

TH = 64
SH = 20
LAT = ("x", "yh")
LON = ("yl", "z", "core")


PLANE = ("x", "yh", "yl")


def shared(value, axes):
    peers = lax.axis_size(axes)
    copies = jnp.broadcast_to(value[None], (peers,) + value.shape)
    return lax.all_to_all(copies, axes, 0, 0)


def summed(value):
    swap = [(0, 1), (1, 0)]
    core = lax.axis_index("core")
    rows, cols = value.shape
    half = rows // 2
    kept = lax.dynamic_slice_in_dim(value, core * half, half, 0)
    given = lax.dynamic_slice_in_dim(value, (1 - core) * half, half, 0)
    kept = kept + lax.ppermute(given, "core", swap)
    peers = lax.axis_size(PLANE)
    pieces = lax.all_to_all(kept.reshape(peers, half // peers, cols), PLANE, 0, 0)
    piece = shared(pieces.sum(axis=0), ("z",)).sum(axis=0)
    kept = shared(piece, PLANE).reshape(half, cols)
    given = lax.ppermute(kept, "core", swap)
    top = jnp.where(core == 0, kept, given)
    bottom = jnp.where(core == 0, given, kept)
    return jnp.concatenate([top, bottom], axis=0)


TILE = 128
STEP = 8

def product(left, right, over):
    return lax.dot_general(
        left,
        right,
        (over, ((), ())),
        precision=lax.Precision.HIGHEST,
        preferred_element_type=jnp.float32,
    )


def wide(value):
    return jnp.broadcast_to(value, (STEP, TILE))


def eliminate(work):
    for top in range(0, TILE, STEP):
        own = work[top:top + STEP, :TILE]
        cols = [wide(own[:, top + j:top + j + 1]) for j in range(STEP)]
        left = {(i, j): wide(cols[j][i:i + 1, :]) for j in range(STEP) for i in range(j + 1)}
        rows = [[wide(work[top + i:top + i + 1, s:s + TILE]) for s in (0, TILE)] for i in range(STEP)]
        root, upper = [], {}
        for j in range(STEP):
            root.append(lax.rsqrt(left[j, j]))
            for i in range(j + 1, STEP):
                upper[j, i] = left[j, i] * root[j]
            for i in range(j + 1, STEP):
                for n in range(i, STEP):
                    left[i, n] = left[i, n] - upper[j, i] * upper[j, n]
        for j in range(STEP):
            rows[j] = [value * root[j] for value in rows[j]]
            for i in range(j + 1, STEP):
                rows[i] = [value - upper[j, i] * done for value, done in zip(rows[i], rows[j])]
        for j in range(STEP):
            for half in range(2):
                work[top + j:top + j + 1, half * TILE:(half + 1) * TILE] = rows[j][half][:1, :]
        for below in range(top + STEP, TILE, STEP):
            parts = [work[below:below + STEP, s:s + TILE] for s in (0, TILE)]
            factors = [wide(parts[0][:, top + j:top + j + 1]) for j in range(STEP)]
            for j in range(STEP):
                factors[j] = factors[j] * root[j]
                for i in range(j + 1, STEP):
                    factors[i] = factors[i] - upper[j, i] * factors[j]
            for j in range(STEP):
                parts = [value - factors[j] * done for value, done in zip(parts, rows[j])]
            for half in range(2):
                work[below:below + STEP, half * TILE:(half + 1) * TILE] = parts[half]


ROWS = ((0,), (0,))
COLS = ((1,), (1,))
PLAIN = ((1,), (0,))


def factor_kernel(cells, gram, matrix, basis, merged, work):
    row = lax.broadcasted_iota(jnp.int32, (TILE, TILE), 0)
    col = lax.broadcasted_iota(jnp.int32, (TILE, TILE), 1)
    eye = jnp.where(row == col, 1.0, 0.0).astype(jnp.float32)
    scale = float(cells) ** 0.5

    def solve(block):
        work[:, :TILE] = block
        work[:, TILE:] = eye
        eliminate(work)
        upper = jnp.where(row <= col, work[:, :TILE], 0.0)
        lower = jnp.where(row >= col, work[:, TILE:], 0.0)
        return upper, lower

    r11, w11 = solve(gram[:TILE, :TILE])
    r12 = product(w11, gram[:TILE, TILE:], PLAIN)
    r22, w22 = solve(gram[TILE:, TILE:] - product(r12, r12, ROWS))
    w21 = -product(w22, product(r12, w11, ROWS), PLAIN)
    merged[:TILE, :TILE] = r11 * (1.0 / scale)
    merged[:TILE, TILE:] = r12 * (1.0 / scale)
    merged[TILE:, :TILE] = jnp.zeros((TILE, TILE), jnp.float32)
    merged[TILE:, TILE:] = r22 * (1.0 / scale)
    first, second = (matrix[:, :TILE], matrix[:, TILE:])
    left = product(first, w11 * scale, COLS)
    right = product(first, w21 * scale, COLS) + product(second, w22 * scale, COLS)
    lines, side, _ = basis.shape
    for line in range(lines):
        part = slice(line * side, (line + 1) * side)
        basis[line, :, :TILE] = left[part]
        basis[line, :, TILE:] = right[part]


def shifted(kernel, rows, start):
    flat = jnp.concatenate([kernel, jnp.zeros((1, TILE - kernel.shape[1]), jnp.float32)], axis=1)
    return pltpu.roll(jnp.broadcast_to(flat, (rows, TILE)), start, 1, stride=1, stride_axis=0)


def smoother(kernel, side):
    pair = 2 * side
    row = lax.broadcasted_iota(jnp.int32, (pair, TILE), 0)
    lane = lax.broadcasted_iota(jnp.int32, (pair, TILE), 1)
    total = jnp.zeros((pair, TILE), jnp.float32)
    for part in range(3):
        place = lane - part * pair
        inside = (place >= 0) & (place < pair) & ((place >= side) == (row >= side))
        total = jnp.where(inside, shifted(kernel, pair, part * side), total)
    return total[:, : 3 * pair]


def stacked(before, own, after, first, count):
    part = slice(first, first + count)
    halves = range(own.shape[0])
    return jnp.concatenate(
        [
            jnp.concatenate([lines[half, part, :] for half in halves], axis=1)
            for lines in (before, own, after)
        ],
        axis=0,
    )


def turned(out, line, side, value):
    for half in range(out.shape[0]):
        out.at[half][pl.ds(line, side, stride=out.shape[1] // side), :] = value[
            :, half * TILE : (half + 1) * TILE
        ]


def filter_kernel(taps, field, out, padded):
    rows, cols, hours = field.shape
    steps = out.shape[0] * TILE
    count = taps.shape[1]
    lane = lax.broadcasted_iota(jnp.int32, (1, count), 1)
    full = taps[...] + jnp.where(lane == TH, 1.0, 0.0)
    full = jnp.concatenate([full, jnp.zeros((1, hours - count), jnp.float32)], axis=1)
    skew = pltpu.roll(jnp.broadcast_to(full, (steps, hours)), 0, 1, stride=1, stride_axis=0)
    padded[...] = jnp.zeros_like(padded)
    padded[:, :cols, :] = field[...]
    stride = padded.shape[1]
    result = product(padded[...].reshape(rows * stride, hours), skew, COLS)
    for row in range(rows):
        turned(out, row, cols, result[row * stride : row * stride + cols])


def lat_kernel_body(side, kernel, before, own, after, out):
    band = smoother(kernel[...], side)
    pair = 2 * side
    for first in range(0, own.shape[1], pair):
        result = product(band, stacked(before, own, after, first, pair), PLAIN)
        for line in range(2):
            turned(out, first // side + line, side, result[line * side : (line + 1) * side])


def lon_kernel_body(side, weights, kernel, before, own, after, out, gram):
    band = smoother(kernel[...], side)
    pair = 2 * side
    row = lax.broadcasted_iota(jnp.int32, (pair, 1), 0)
    for first in range(0, own.shape[1], pair):
        line = first // side
        weight = jnp.where(row < side, weights[line], weights[line + 1])
        result = product(band, stacked(before, own, after, first, pair), PLAIN)
        out[first : first + pair, :] = result * weight
    gram[...] = product(out[...], out[...], ROWS)


def called(kernel, name, shapes, scratch, scalars, *args):
    spaces = [pltpu.SMEM] * scalars + [pltpu.VMEM] * (len(args) - scalars)
    return pl.pallas_call(
        kernel,
        out_shape=[jax.ShapeDtypeStruct(shape, jnp.float32) for shape in shapes],
        in_specs=[pl.BlockSpec(memory_space=space) for space in spaces],
        out_specs=[pl.BlockSpec(memory_space=pltpu.VMEM)] * len(shapes),
        scratch_shapes=scratch,
        compiler_params=pltpu.CompilerParams(vmem_limit_bytes=24 * 1024 * 1024),
        name=name,
    )(*args)


def neighbours(value, axes, wrap):
    peers = lax.axis_size(axes)
    up = [(i, (i + 1) % peers) for i in range(peers if wrap else peers - 1)]
    down = [(j, i) for i, j in up]
    return lax.ppermute(value, axes, up), lax.ppermute(value, axes, down)


def body(field, lat_kernel, lon_kernel, time_taps):
    rows_lat, rows_lon, length_in = field.shape
    steps_out = length_in - 2 * TH
    lat_place = lax.axis_index(LAT)
    total_lat = rows_lat * lax.axis_size(LAT)
    local = rows_lat * rows_lon
    cells = local * lax.axis_size(LAT) * lax.axis_size(LON)
    tall = -(-rows_lon // STEP) * STEP
    globrow = (lat_place * rows_lat + jnp.arange(rows_lat, dtype=jnp.int32)).astype(jnp.float32)
    latitude = jnp.pi * (globrow + 0.5) / total_lat - jnp.pi / 2
    weights = jnp.sqrt(jnp.cos(latitude))
    flat = (local, steps_out)
    halves = (steps_out // TILE, local, TILE)
    (filtered,) = called(
        filter_kernel,
        "filter",
        [halves],
        [pltpu.VMEM((rows_lat, tall, length_in), jnp.float32)],
        0,
        time_taps[None],
        field,
    )
    before, after = neighbours(filtered, LAT, False)
    (lat_done,) = called(
        functools.partial(lat_kernel_body, SH), "lat", [halves], [], 0, lat_kernel[None], before, filtered, after
    )
    before, after = neighbours(lat_done, LON, True)
    matrix, local_gram = called(
        functools.partial(lon_kernel_body, SH),
        "lon",
        [flat, (steps_out, steps_out)],
        [],
        1,
        weights,
        lon_kernel[None],
        before,
        lat_done,
        after,
    )
    gram = summed(local_gram)
    basis, merged = called(
        functools.partial(factor_kernel, cells),
        "factor",
        [(rows_lat, rows_lon, steps_out), (steps_out, steps_out)],
        [pltpu.VMEM((TILE, 2 * TILE), jnp.float32)],
        0,
        gram,
        matrix,
    )
    return (basis, merged)


def solution(mesh):
    fine = jax.sharding.Mesh(mesh.devices.reshape(4, 2, 2, 8, 2), ("x", "yh", "yl", "z", "core"))
    placed = (P(LAT, LON, None), P(), P(), P())
    return jax.shard_map(
        body, mesh=fine, in_specs=placed, out_specs=(P(LAT, LON, None), P()), check_vma=False
    )
```

```python
import functools

import jax
import jax.numpy as jnp
from jax import lax
from jax.experimental import pallas as pl
from jax.experimental.pallas import tpu as pltpu
from jax.sharding import PartitionSpec as P

TH = 64
SH = 20
LAT = ("x", "yh")
LON = ("yl", "z", "core")


PLANE = ("x", "yh", "yl")


def shared(value, axes):
    peers = lax.axis_size(axes)
    copies = jnp.broadcast_to(value[None], (peers,) + value.shape)
    return lax.all_to_all(copies, axes, 0, 0)


def summed(value):
    swap = [(0, 1), (1, 0)]
    core = lax.axis_index("core")
    rows, cols = value.shape
    half = rows // 2
    kept = lax.dynamic_slice_in_dim(value, core * half, half, 0)
    given = lax.dynamic_slice_in_dim(value, (1 - core) * half, half, 0)
    kept = kept + lax.ppermute(given, "core", swap)
    peers = lax.axis_size(PLANE)
    pieces = lax.all_to_all(kept.reshape(peers, half // peers, cols), PLANE, 0, 0)
    piece = shared(pieces.sum(axis=0), ("z",)).sum(axis=0)
    kept = shared(piece, PLANE).reshape(half, cols)
    given = lax.ppermute(kept, "core", swap)
    top = jnp.where(core == 0, kept, given)
    bottom = jnp.where(core == 0, given, kept)
    return jnp.concatenate([top, bottom], axis=0)


TILE = 128
STEP = 8

def product(left, right, over):
    return lax.dot_general(
        left,
        right,
        (over, ((), ())),
        precision=lax.Precision.HIGHEST,
        preferred_element_type=jnp.float32,
    )


def wide(value):
    return jnp.broadcast_to(value, (STEP, TILE))


def eliminate(work):
    for top in range(0, TILE, STEP):
        own = work[top:top + STEP, :TILE]
        cols = [wide(own[:, top + j:top + j + 1]) for j in range(STEP)]
        left = {(i, j): wide(cols[j][i:i + 1, :]) for j in range(STEP) for i in range(j + 1)}
        rows = [[wide(work[top + i:top + i + 1, s:s + TILE]) for s in (0, TILE)] for i in range(STEP)]
        root, upper = [], {}
        for j in range(STEP):
            root.append(lax.rsqrt(left[j, j]))
            for i in range(j + 1, STEP):
                upper[j, i] = left[j, i] * root[j]
            for i in range(j + 1, STEP):
                for n in range(i, STEP):
                    left[i, n] = left[i, n] - upper[j, i] * upper[j, n]
        for j in range(STEP):
            rows[j] = [value * root[j] for value in rows[j]]
            for i in range(j + 1, STEP):
                rows[i] = [value - upper[j, i] * done for value, done in zip(rows[i], rows[j])]
        for j in range(STEP):
            for half in range(2):
                work[top + j:top + j + 1, half * TILE:(half + 1) * TILE] = rows[j][half][:1, :]
        for below in range(top + STEP, TILE, STEP):
            parts = [work[below:below + STEP, s:s + TILE] for s in (0, TILE)]
            factors = [wide(parts[0][:, top + j:top + j + 1]) for j in range(STEP)]
            for j in range(STEP):
                factors[j] = factors[j] * root[j]
                for i in range(j + 1, STEP):
                    factors[i] = factors[i] - upper[j, i] * factors[j]
            for j in range(STEP):
                parts = [value - factors[j] * done for value, done in zip(parts, rows[j])]
            for half in range(2):
                work[below:below + STEP, half * TILE:(half + 1) * TILE] = parts[half]


ROWS = ((0,), (0,))
COLS = ((1,), (1,))
PLAIN = ((1,), (0,))


def factor_kernel(cells, gram, matrix, basis, merged, work):
    row = lax.broadcasted_iota(jnp.int32, (TILE, TILE), 0)
    col = lax.broadcasted_iota(jnp.int32, (TILE, TILE), 1)
    eye = jnp.where(row == col, 1.0, 0.0).astype(jnp.float32)
    scale = float(cells) ** 0.5

    def solve(block):
        work[:, :TILE] = block
        work[:, TILE:] = eye
        eliminate(work)
        upper = jnp.where(row <= col, work[:, :TILE], 0.0)
        lower = jnp.where(row >= col, work[:, TILE:], 0.0)
        return upper, lower

    r11, w11 = solve(gram[:TILE, :TILE])
    r12 = product(w11, gram[:TILE, TILE:], PLAIN)
    r22, w22 = solve(gram[TILE:, TILE:] - product(r12, r12, ROWS))
    w21 = -product(w22, product(r12, w11, ROWS), PLAIN)
    merged[:TILE, :TILE] = r11 * (1.0 / scale)
    merged[:TILE, TILE:] = r12 * (1.0 / scale)
    merged[TILE:, :TILE] = jnp.zeros((TILE, TILE), jnp.float32)
    merged[TILE:, TILE:] = r22 * (1.0 / scale)
    first, second = (matrix[:, :TILE], matrix[:, TILE:])
    left = product(first, w11 * scale, COLS)
    right = product(first, w21 * scale, COLS) + product(second, w22 * scale, COLS)
    lines, side, _ = basis.shape
    for line in range(lines):
        part = slice(line * side, (line + 1) * side)
        basis[line, :, :TILE] = left[part]
        basis[line, :, TILE:] = right[part]


def shifted(kernel, rows, start):
    flat = jnp.concatenate([kernel, jnp.zeros((1, TILE - kernel.shape[1]), jnp.float32)], axis=1)
    return pltpu.roll(jnp.broadcast_to(flat, (rows, TILE)), start, 1, stride=1, stride_axis=0)


def smoother(kernel, side):
    pair = 2 * side
    row = lax.broadcasted_iota(jnp.int32, (pair, TILE), 0)
    lane = lax.broadcasted_iota(jnp.int32, (pair, TILE), 1)
    total = jnp.zeros((pair, TILE), jnp.float32)
    for part in range(3):
        place = lane - part * pair
        inside = (place >= 0) & (place < pair) & ((place >= side) == (row >= side))
        total = jnp.where(inside, shifted(kernel, pair, part * side), total)
    return total[:, : 3 * pair]


def stacked(before, own, after, first, count):
    part = slice(first, first + count)
    return jnp.concatenate([lines[part, :] for lines in (before, own, after)], axis=0)


def turned(out, line, side, value):
    out[pl.ds(line, side, stride=out.shape[0] // side), :] = value


def filter_kernel(taps, field, first, second, padded):
    rows, cols, hours = field.shape
    steps = 2 * TILE
    count = taps.shape[1]
    lane = lax.broadcasted_iota(jnp.int32, (1, count), 1)
    full = taps[...] + jnp.where(lane == TH, 1.0, 0.0)
    full = jnp.concatenate([full, jnp.zeros((1, hours - count), jnp.float32)], axis=1)
    skew = pltpu.roll(jnp.broadcast_to(full, (steps, hours)), 0, 1, stride=1, stride_axis=0)
    padded[...] = jnp.zeros_like(padded)
    padded[:, :cols, :] = field[...]
    stride = padded.shape[1]
    result = product(padded[...].reshape(rows * stride, hours), skew, COLS)
    for row in range(rows):
        line = slice(row * stride, row * stride + cols)
        turned(first, row, cols, result[line, :TILE])
        turned(second, row, cols, result[line, TILE:])


def lat_kernel_body(side, low, kernel, near, own, far, out):
    pair = 2 * side
    plain = smoother(kernel[...], side)
    lead, middle, trail = (plain[:, at : at + pair] for at in (0, pair, 2 * pair))
    swapped = jnp.concatenate([trail, middle, lead], axis=1)
    band = jnp.where(low[0] == 1, swapped, plain)
    for first in range(0, own.shape[0], pair):
        result = product(band, stacked(near, own, far, first, pair), PLAIN)
        for line in range(2):
            turned(out, first // side + line, side, result[line * side : (line + 1) * side])


def lon_kernel_body(side, weights, kernel, *refs):
    parts, (out, gram) = (refs[:-2], refs[-2:])
    band = smoother(kernel[...], side)
    pair = 2 * side
    row = lax.broadcasted_iota(jnp.int32, (pair, 1), 0)
    for first in range(0, out.shape[0], pair):
        line = first // side
        weight = jnp.where(row < side, weights[line], weights[line + 1])
        cells = [stacked(*parts[at : at + 3], first, pair) for at in (0, 3)]
        result = product(band, jnp.concatenate(cells, axis=1), PLAIN)
        out[first : first + pair, :] = result * weight
    gram[...] = product(out[...], out[...], ROWS)


def called(kernel, name, shapes, scratch, scalars, *args):
    spaces = [pltpu.SMEM] * scalars + [pltpu.VMEM] * (len(args) - scalars)
    return pl.pallas_call(
        kernel,
        out_shape=[jax.ShapeDtypeStruct(shape, jnp.float32) for shape in shapes],
        in_specs=[pl.BlockSpec(memory_space=space) for space in spaces],
        out_specs=[pl.BlockSpec(memory_space=pltpu.VMEM)] * len(shapes),
        scratch_shapes=scratch,
        compiler_params=pltpu.CompilerParams(vmem_limit_bytes=24 * 1024 * 1024),
        name=name,
    )(*args)


def neighbours(value, axes, wrap):
    peers = lax.axis_size(axes)
    up = [(i, (i + 1) % peers) for i in range(peers if wrap else peers - 1)]
    down = [(j, i) for i, j in up]
    return lax.ppermute(value, axes, up), lax.ppermute(value, axes, down)


def passed_on(value):
    spots, halves = (lax.axis_size("x"), lax.axis_size("yh"))
    near = lax.ppermute(value, "yh", [(0, 1), (1, 0)])
    up = [(x * halves, (x + 1) * halves) for x in range(spots - 1)]
    down = [((x + 1) * halves + 1, x * halves + 1) for x in range(spots - 1)]
    return near, lax.ppermute(near, LAT, up + down)


def body(field, lat_kernel, lon_kernel, time_taps):
    rows_lat, rows_lon, length_in = field.shape
    steps_out = length_in - 2 * TH
    lat_place = lax.axis_index(LAT)
    total_lat = rows_lat * lax.axis_size(LAT)
    local = rows_lat * rows_lon
    cells = local * lax.axis_size(LAT) * lax.axis_size(LON)
    tall = -(-rows_lon // STEP) * STEP
    globrow = (lat_place * rows_lat + jnp.arange(rows_lat, dtype=jnp.int32)).astype(jnp.float32)
    latitude = jnp.pi * (globrow + 0.5) / total_lat - jnp.pi / 2
    weights = jnp.sqrt(jnp.cos(latitude))
    flat = (local, steps_out)
    half = (local, TILE)
    filtered = called(
        filter_kernel,
        "filter",
        [half, half],
        [pltpu.VMEM((rows_lat, tall, length_in), jnp.float32)],
        0,
        time_taps[None],
        field,
    )
    low = (lax.axis_index("yh") == 0).astype(jnp.int32)[None]
    parts = []
    for own in filtered:
        near, far = passed_on(own)
        (lat_done,) = called(
            functools.partial(lat_kernel_body, SH), "lat", [half], [], 1, low, lat_kernel[None], near, own, far
        )
        before, after = neighbours(lat_done, LON, True)
        parts += [before, lat_done, after]
    matrix, local_gram = called(
        functools.partial(lon_kernel_body, SH),
        "lon",
        [flat, (steps_out, steps_out)],
        [],
        1,
        weights,
        lon_kernel[None],
        *parts,
    )
    gram = summed(local_gram)
    basis, merged = called(
        functools.partial(factor_kernel, cells),
        "factor",
        [(rows_lat, rows_lon, steps_out), (steps_out, steps_out)],
        [pltpu.VMEM((TILE, 2 * TILE), jnp.float32)],
        0,
        gram,
        matrix,
    )
    return (basis, merged)


def solution(mesh):
    fine = jax.sharding.Mesh(mesh.devices.reshape(4, 2, 2, 8, 2), ("x", "yh", "yl", "z", "core"))
    placed = (P(LAT, LON, None), P(), P(), P())
    return jax.shard_map(
        body, mesh=fine, in_specs=placed, out_specs=(P(LAT, LON, None), P()), check_vma=False
    )
```

```python
import functools

import jax
import jax.numpy as jnp
from jax import lax
from jax.experimental import pallas as pl
from jax.experimental.pallas import tpu as pltpu
from jax.sharding import PartitionSpec as P

TH = 64
SH = 20
LAT = ("x", "yh")
LON = ("yl", "z", "core")


PLANE = ("x", "yh", "yl")


def shared(value, axes):
    peers = lax.axis_size(axes)
    copies = jnp.broadcast_to(value[None], (peers,) + value.shape)
    return lax.all_to_all(copies, axes, 0, 0)


def summed(value):
    swap = [(0, 1), (1, 0)]
    core = lax.axis_index("core")
    rows, cols = value.shape
    half = rows // 2
    kept = lax.dynamic_slice_in_dim(value, core * half, half, 0)
    given = lax.dynamic_slice_in_dim(value, (1 - core) * half, half, 0)
    kept = kept + lax.ppermute(given, "core", swap)
    peers = lax.axis_size(PLANE)
    pieces = lax.all_to_all(kept.reshape(peers, half // peers, cols), PLANE, 0, 0)
    piece = shared(pieces.sum(axis=0), ("z",)).sum(axis=0)
    kept = shared(piece, PLANE).reshape(half, cols)
    given = lax.ppermute(kept, "core", swap)
    top = jnp.where(core == 0, kept, given)
    bottom = jnp.where(core == 0, given, kept)
    return jnp.concatenate([top, bottom], axis=0)


TILE = 128
STEP = 8

def product(left, right, over):
    return lax.dot_general(
        left,
        right,
        (over, ((), ())),
        precision=lax.Precision.HIGHEST,
        preferred_element_type=jnp.float32,
    )


def wide(value):
    return jnp.broadcast_to(value, (STEP, TILE))


def eliminate(work):
    for top in range(0, TILE, STEP):
        own = work[top:top + STEP, :TILE]
        cols = [wide(own[:, top + j:top + j + 1]) for j in range(STEP)]
        left = {(i, j): wide(cols[j][i:i + 1, :]) for j in range(STEP) for i in range(j + 1)}
        rows = [[wide(work[top + i:top + i + 1, s:s + TILE]) for s in (0, TILE)] for i in range(STEP)]
        root, upper = [], {}
        for j in range(STEP):
            root.append(lax.rsqrt(left[j, j]))
            for i in range(j + 1, STEP):
                upper[j, i] = left[j, i] * root[j]
            for i in range(j + 1, STEP):
                for n in range(i, STEP):
                    left[i, n] = left[i, n] - upper[j, i] * upper[j, n]
        for j in range(STEP):
            rows[j] = [value * root[j] for value in rows[j]]
            for i in range(j + 1, STEP):
                rows[i] = [value - upper[j, i] * done for value, done in zip(rows[i], rows[j])]
        for j in range(STEP):
            for half in range(2):
                work[top + j:top + j + 1, half * TILE:(half + 1) * TILE] = rows[j][half][:1, :]
        for below in range(top + STEP, TILE, STEP):
            parts = [work[below:below + STEP, s:s + TILE] for s in (0, TILE)]
            factors = [wide(parts[0][:, top + j:top + j + 1]) for j in range(STEP)]
            for j in range(STEP):
                factors[j] = factors[j] * root[j]
                for i in range(j + 1, STEP):
                    factors[i] = factors[i] - upper[j, i] * factors[j]
            for j in range(STEP):
                parts = [value - factors[j] * done for value, done in zip(parts, rows[j])]
            for half in range(2):
                work[below:below + STEP, half * TILE:(half + 1) * TILE] = parts[half]


ROWS = ((0,), (0,))
COLS = ((1,), (1,))
PLAIN = ((1,), (0,))


def factor_kernel(cells, gram, matrix, basis, merged, work):
    row = lax.broadcasted_iota(jnp.int32, (TILE, TILE), 0)
    col = lax.broadcasted_iota(jnp.int32, (TILE, TILE), 1)
    eye = jnp.where(row == col, 1.0, 0.0).astype(jnp.float32)
    scale = float(cells) ** 0.5

    def solve(block):
        work[:, :TILE] = block
        work[:, TILE:] = eye
        eliminate(work)
        upper = jnp.where(row <= col, work[:, :TILE], 0.0)
        lower = jnp.where(row >= col, work[:, TILE:], 0.0)
        return upper, lower

    r11, w11 = solve(gram[:TILE, :TILE])
    r12 = product(w11, gram[:TILE, TILE:], PLAIN)
    r22, w22 = solve(gram[TILE:, TILE:] - product(r12, r12, ROWS))
    w21 = -product(w22, product(r12, w11, ROWS), PLAIN)
    merged[:TILE, :TILE] = r11 * (1.0 / scale)
    merged[:TILE, TILE:] = r12 * (1.0 / scale)
    merged[TILE:, :TILE] = jnp.zeros((TILE, TILE), jnp.float32)
    merged[TILE:, TILE:] = r22 * (1.0 / scale)
    first, second = (matrix[:, :TILE], matrix[:, TILE:])
    left = product(first, w11 * scale, COLS)
    right = product(first, w21 * scale, COLS) + product(second, w22 * scale, COLS)
    lines, side, _ = basis.shape
    for line in range(lines):
        part = slice(line * side, (line + 1) * side)
        basis[line, :, :TILE] = left[part]
        basis[line, :, TILE:] = right[part]


def shifted(kernel, rows, start):
    flat = jnp.concatenate([kernel, jnp.zeros((1, TILE - kernel.shape[1]), jnp.float32)], axis=1)
    return pltpu.roll(jnp.broadcast_to(flat, (rows, TILE)), start, 1, stride=1, stride_axis=0)


def smoother(kernel, side):
    pair = 2 * side
    row = lax.broadcasted_iota(jnp.int32, (pair, TILE), 0)
    lane = lax.broadcasted_iota(jnp.int32, (pair, TILE), 1)
    total = jnp.zeros((pair, TILE), jnp.float32)
    for part in range(3):
        place = lane - part * pair
        inside = (place >= 0) & (place < pair) & ((place >= side) == (row >= side))
        total = jnp.where(inside, shifted(kernel, pair, part * side), total)
    return total[:, : 3 * pair]


def stacked(before, own, after, first, count):
    part = slice(first, first + count)
    return jnp.concatenate([lines[part, :] for lines in (before, own, after)], axis=0)


def turned(out, line, side, value):
    out[pl.ds(line, side, stride=out.shape[0] // side), :] = value


def filter_kernel(taps, field, first, second, padded):
    rows, cols, hours = field.shape
    steps = 2 * TILE
    count = taps.shape[1]
    lane = lax.broadcasted_iota(jnp.int32, (1, count), 1)
    full = taps[...] + jnp.where(lane == TH, 1.0, 0.0)
    full = jnp.concatenate([full, jnp.zeros((1, hours - count), jnp.float32)], axis=1)
    skew = pltpu.roll(jnp.broadcast_to(full, (steps, hours)), 0, 1, stride=1, stride_axis=0)
    padded[...] = jnp.zeros_like(padded)
    padded[:, :cols, :] = field[...]
    stride = padded.shape[1]
    result = product(padded[...].reshape(rows * stride, hours), skew, COLS)
    for row in range(rows):
        line = slice(row * stride, row * stride + cols)
        turned(first, row, cols, result[line, :TILE])
        turned(second, row, cols, result[line, TILE:])


def ordered(first, kernel, side):
    pair = 2 * side
    plain = smoother(kernel[...], side)
    lead, middle, trail = (plain[:, at : at + pair] for at in (0, pair, 2 * pair))
    swapped = jnp.concatenate([trail, middle, lead], axis=1)
    return jnp.where(first[0] == 1, swapped, plain)


def lat_kernel_body(side, low, kernel, *refs):
    parts, out = (refs[:-1], refs[-1])
    band = ordered(low, kernel, side)
    pair = 2 * side
    for half in range(out.shape[0]):
        lines = parts[3 * half : 3 * half + 3]
        for first in range(0, out.shape[1], pair):
            result = product(band, stacked(*lines, first, pair), PLAIN)
            for line in range(2):
                part = result[line * side : (line + 1) * side]
                turned(out.at[half], first // side + line, side, part)


def lon_kernel_body(side, weights, low, kernel, near, own, far, out, gram):
    band = ordered(low, kernel, side)
    pair = 2 * side
    row = lax.broadcasted_iota(jnp.int32, (pair, 1), 0)
    for first in range(0, out.shape[0], pair):
        line = first // side
        weight = jnp.where(row < side, weights[line], weights[line + 1])
        cells = [stacked(near.at[at], own.at[at], far.at[at], first, pair) for at in range(2)]
        result = product(band, jnp.concatenate(cells, axis=1), PLAIN)
        out[first : first + pair, :] = result * weight
    gram[...] = product(out[...], out[...], ROWS)


def called(kernel, name, shapes, scratch, scalars, *args):
    spaces = [pltpu.SMEM] * scalars + [pltpu.VMEM] * (len(args) - scalars)
    return pl.pallas_call(
        kernel,
        out_shape=[jax.ShapeDtypeStruct(shape, jnp.float32) for shape in shapes],
        in_specs=[pl.BlockSpec(memory_space=space) for space in spaces],
        out_specs=[pl.BlockSpec(memory_space=pltpu.VMEM)] * len(shapes),
        scratch_shapes=scratch,
        compiler_params=pltpu.CompilerParams(vmem_limit_bytes=24 * 1024 * 1024),
        name=name,
    )(*args)


def around(value):
    peers = lax.axis_size(LON)
    near = lax.ppermute(value, "core", [(0, 1), (1, 0)])
    across = [(i, (i + 1) % peers) for i in range(1, peers, 2)]
    return near, lax.ppermute(value, LON, across + [(j, i) for i, j in across])


def passed_on(value):
    spots, halves = (lax.axis_size("x"), lax.axis_size("yh"))
    near = lax.ppermute(value, "yh", [(0, 1), (1, 0)])
    up = [(x * halves, (x + 1) * halves) for x in range(spots - 1)]
    down = [((x + 1) * halves + 1, x * halves + 1) for x in range(spots - 1)]
    return near, lax.ppermute(near, LAT, up + down)


def body(field, lat_kernel, lon_kernel, time_taps):
    rows_lat, rows_lon, length_in = field.shape
    steps_out = length_in - 2 * TH
    lat_place = lax.axis_index(LAT)
    total_lat = rows_lat * lax.axis_size(LAT)
    local = rows_lat * rows_lon
    cells = local * lax.axis_size(LAT) * lax.axis_size(LON)
    tall = -(-rows_lon // STEP) * STEP
    globrow = (lat_place * rows_lat + jnp.arange(rows_lat, dtype=jnp.int32)).astype(jnp.float32)
    latitude = jnp.pi * (globrow + 0.5) / total_lat - jnp.pi / 2
    weights = jnp.sqrt(jnp.cos(latitude))
    flat = (local, steps_out)
    half = (local, TILE)
    filtered = called(
        filter_kernel,
        "filter",
        [half, half],
        [pltpu.VMEM((rows_lat, tall, length_in), jnp.float32)],
        0,
        time_taps[None],
        field,
    )
    low = (lax.axis_index("yh") == 0).astype(jnp.int32)[None]
    parts = []
    for own in filtered:
        near, far = passed_on(own)
        parts += [near, own, far]
    (lat_done,) = called(
        functools.partial(lat_kernel_body, SH), "lat", [(2, local, TILE)], [], 1, low, lat_kernel[None], *parts
    )
    near, far = around(lat_done)
    matrix, local_gram = called(
        functools.partial(lon_kernel_body, SH),
        "lon",
        [flat, (steps_out, steps_out)],
        [],
        2,
        weights,
        (lax.axis_index("core") == 0).astype(jnp.int32)[None],
        lon_kernel[None],
        near,
        lat_done,
        far,
    )
    gram = summed(local_gram)
    basis, merged = called(
        functools.partial(factor_kernel, cells),
        "factor",
        [(rows_lat, rows_lon, steps_out), (steps_out, steps_out)],
        [pltpu.VMEM((TILE, 2 * TILE), jnp.float32)],
        0,
        gram,
        matrix,
    )
    return (basis, merged)


def solution(mesh):
    fine = jax.sharding.Mesh(mesh.devices.reshape(4, 2, 2, 8, 2), ("x", "yh", "yl", "z", "core"))
    placed = (P(LAT, LON, None), P(), P(), P())
    return jax.shard_map(
        body, mesh=fine, in_specs=placed, out_specs=(P(LAT, LON, None), P()), check_vma=False
    )
```

```python
import functools

import jax
import jax.numpy as jnp
from jax import lax
from jax.experimental import pallas as pl
from jax.experimental.pallas import tpu as pltpu
from jax.sharding import PartitionSpec as P

TH = 64
SH = 20
LAT = ("x", "yh")
LON = ("yl", "z", "core")


PLANE = ("x", "yh", "yl")


def shared(value, axes):
    peers = lax.axis_size(axes)
    copies = jnp.broadcast_to(value[None], (peers,) + value.shape)
    return lax.all_to_all(copies, axes, 0, 0)


def summed(value):
    swap = [(0, 1), (1, 0)]
    core = lax.axis_index("core")
    rows, cols = value.shape
    half = rows // 2
    kept = lax.dynamic_slice_in_dim(value, core * half, half, 0)
    given = lax.dynamic_slice_in_dim(value, (1 - core) * half, half, 0)
    kept = kept + lax.ppermute(given, "core", swap)
    peers = lax.axis_size(PLANE)
    pieces = lax.all_to_all(kept.reshape(peers, half // peers, cols), PLANE, 0, 0)
    piece = shared(pieces.sum(axis=0), ("z",)).sum(axis=0)
    kept = shared(piece, PLANE).reshape(half, cols)
    given = lax.ppermute(kept, "core", swap)
    top = jnp.where(core == 0, kept, given)
    bottom = jnp.where(core == 0, given, kept)
    return jnp.concatenate([top, bottom], axis=0)


TILE = 128
STEP = 8

def product(left, right, over):
    return lax.dot_general(
        left,
        right,
        (over, ((), ())),
        precision=lax.Precision.HIGHEST,
        preferred_element_type=jnp.float32,
    )


def wide(value):
    return jnp.broadcast_to(value, (STEP, TILE))


def eliminate(work):
    for top in range(0, TILE, STEP):
        own = work[top:top + STEP, :TILE]
        cols = [wide(own[:, top + j:top + j + 1]) for j in range(STEP)]
        left = {(i, j): wide(cols[j][i:i + 1, :]) for j in range(STEP) for i in range(j + 1)}
        rows = [[wide(work[top + i:top + i + 1, s:s + TILE]) for s in (0, TILE)] for i in range(STEP)]
        root, upper = [], {}
        for j in range(STEP):
            root.append(lax.rsqrt(left[j, j]))
            for i in range(j + 1, STEP):
                upper[j, i] = left[j, i] * root[j]
            for i in range(j + 1, STEP):
                for n in range(i, STEP):
                    left[i, n] = left[i, n] - upper[j, i] * upper[j, n]
        for j in range(STEP):
            rows[j] = [value * root[j] for value in rows[j]]
            for i in range(j + 1, STEP):
                rows[i] = [value - upper[j, i] * done for value, done in zip(rows[i], rows[j])]
        for j in range(STEP):
            for half in range(2):
                work[top + j:top + j + 1, half * TILE:(half + 1) * TILE] = rows[j][half][:1, :]
        for below in range(top + STEP, TILE, STEP):
            parts = [work[below:below + STEP, s:s + TILE] for s in (0, TILE)]
            factors = [wide(parts[0][:, top + j:top + j + 1]) for j in range(STEP)]
            for j in range(STEP):
                factors[j] = factors[j] * root[j]
                for i in range(j + 1, STEP):
                    factors[i] = factors[i] - upper[j, i] * factors[j]
            for j in range(STEP):
                parts = [value - factors[j] * done for value, done in zip(parts, rows[j])]
            for half in range(2):
                work[below:below + STEP, half * TILE:(half + 1) * TILE] = parts[half]


ROWS = ((0,), (0,))
COLS = ((1,), (1,))
PLAIN = ((1,), (0,))


def factor_kernel(cells, gram, matrix, basis, merged, work):
    row = lax.broadcasted_iota(jnp.int32, (TILE, TILE), 0)
    col = lax.broadcasted_iota(jnp.int32, (TILE, TILE), 1)
    eye = jnp.where(row == col, 1.0, 0.0).astype(jnp.float32)
    scale = float(cells) ** 0.5

    def solve(block):
        work[:, :TILE] = block
        work[:, TILE:] = eye
        eliminate(work)
        upper = jnp.where(row <= col, work[:, :TILE], 0.0)
        lower = jnp.where(row >= col, work[:, TILE:], 0.0)
        return upper, lower

    r11, w11 = solve(gram[:TILE, :TILE])
    r12 = product(w11, gram[:TILE, TILE:], PLAIN)
    r22, w22 = solve(gram[TILE:, TILE:] - product(r12, r12, ROWS))
    w21 = -product(w22, product(r12, w11, ROWS), PLAIN)
    merged[:TILE, :TILE] = r11 * (1.0 / scale)
    merged[:TILE, TILE:] = r12 * (1.0 / scale)
    merged[TILE:, :TILE] = jnp.zeros((TILE, TILE), jnp.float32)
    merged[TILE:, TILE:] = r22 * (1.0 / scale)
    first, second = (matrix[0], matrix[1])
    left = product(first, w11 * scale, COLS)
    right = product(first, w21 * scale, COLS) + product(second, w22 * scale, COLS)
    lines, side, _ = basis.shape
    for line in range(lines):
        part = slice(line * side, (line + 1) * side)
        basis[line, :, :TILE] = left[part]
        basis[line, :, TILE:] = right[part]


def shifted(kernel, rows, start):
    flat = jnp.concatenate([kernel, jnp.zeros((1, TILE - kernel.shape[1]), jnp.float32)], axis=1)
    return pltpu.roll(jnp.broadcast_to(flat, (rows, TILE)), start, 1, stride=1, stride_axis=0)


def smoother(kernel, side):
    pair = 2 * side
    row = lax.broadcasted_iota(jnp.int32, (pair, TILE), 0)
    lane = lax.broadcasted_iota(jnp.int32, (pair, TILE), 1)
    total = jnp.zeros((pair, TILE), jnp.float32)
    for part in range(3):
        place = lane - part * pair
        inside = (place >= 0) & (place < pair) & ((place >= side) == (row >= side))
        total = jnp.where(inside, shifted(kernel, pair, part * side), total)
    return total[:, : 3 * pair]


def stacked(before, own, after, first, count):
    part = slice(first, first + count)
    return jnp.concatenate([lines[part, :] for lines in (before, own, after)], axis=0)


def turned(out, line, side, value):
    out[pl.ds(line, side, stride=out.shape[0] // side), :] = value


def ordered(first, kernel, side):
    pair = 2 * side
    plain = smoother(kernel[...], side)
    lead, middle, trail = (plain[:, at : at + pair] for at in (0, pair, 2 * pair))
    swapped = jnp.concatenate([trail, middle, lead], axis=1)
    return jnp.where(first == 1, swapped, plain)


def bands_kernel(side, low, weights, lat_kernel, lon_kernel, lat_band, lon_band, lat_weighted):
    lat_band[...] = ordered(low[0], lat_kernel, side)
    lon_band[...] = ordered(low[1], lon_kernel, side)
    row = lax.broadcasted_iota(jnp.int32, (2 * side, 1), 0)
    weight = jnp.zeros((2 * side, 1), jnp.float32)
    for line in range(side):
        weight = jnp.where((row == line) | (row == side + line), weights[line], weight)
    lat_weighted[...] = lat_band[...] * weight


def filter_kernel(lines, taps, field, first, second, staged, padded, arrived):
    rows, cols, hours = field.shape
    stride = padded.shape[1]
    parts = [pl.ds(row, lines) for row in range(0, rows, lines)]
    copies = [
        pltpu.make_async_copy(field.at[part], staged.at[part], arrived.at[at])
        for at, part in enumerate(parts)
    ]
    for copy in copies:
        copy.start()
    padded[:, cols:, :] = jnp.zeros((rows, stride - cols, hours), jnp.float32)
    count = taps.shape[1]
    lane = lax.broadcasted_iota(jnp.int32, (1, count), 1)
    full = taps[...] + jnp.where(lane == TH, 1.0, 0.0)
    full = jnp.concatenate([full, jnp.zeros((1, hours - count), jnp.float32)], axis=1)
    skew = pltpu.roll(jnp.broadcast_to(full, (2 * TILE, hours)), 0, 1, stride=1, stride_axis=0)
    for at, copy in enumerate(copies):
        copy.wait()
        part = slice(at * lines, (at + 1) * lines)
        padded[part, :cols, :] = staged[part]
        part = padded[part].reshape(lines * stride, hours)
        result = product(part, skew, COLS)
        for line in range(lines):
            row = at * lines + line
            value = result[line * stride : line * stride + cols]
            turned(first, row, cols, value[:, :TILE])
            second[row * cols : (row + 1) * cols, :] = value[:, TILE:]


def smooth_kernel(side, band, near, own, far, out):
    pair = 2 * side
    for first in range(0, out.shape[0], pair):
        result = product(band[...], stacked(near, own, far, first, pair), PLAIN)
        for line in range(2):
            turned(out, first // side + line, side, result[line * side : (line + 1) * side])


def last_kernel(side, weights, lon_band, lat_band, *refs):
    parts, (out, gram) = (refs[:-2], refs[-2:])
    pair = 2 * side
    row = lax.broadcasted_iota(jnp.int32, (pair, 1), 0)
    for first in range(0, out.shape[1], pair):
        line = first // side
        weight = jnp.where(row < side, weights[line], weights[line + 1])
        result = product(lon_band[...], stacked(*parts[:3], first, pair), PLAIN)
        out[0, first : first + pair, :] = result * weight
        result = product(lat_band[...], stacked(*parts[3:], first, pair), PLAIN)
        for at in range(2):
            turned(out.at[1], line + at, side, result[at * side : (at + 1) * side])
    both = jnp.concatenate([out[0], out[1]], axis=1)
    gram[...] = product(both, both, ROWS)


def called(kernel, name, shapes, spaces, scratch, *args, mib=24):
    spaces = list(spaces) + [pltpu.VMEM] * (len(args) - len(spaces))
    return pl.pallas_call(
        kernel,
        out_shape=[jax.ShapeDtypeStruct(shape, jnp.float32) for shape in shapes],
        in_specs=[pl.BlockSpec(memory_space=space) for space in spaces],
        out_specs=[pl.BlockSpec(memory_space=pltpu.VMEM)] * len(shapes),
        scratch_shapes=scratch,
        compiler_params=pltpu.CompilerParams(vmem_limit_bytes=mib * 1024 * 1024),
        name=name,
    )(*args)


def around(value):
    peers = lax.axis_size(LON)
    near = lax.ppermute(value, "core", [(0, 1), (1, 0)])
    across = [(i, (i + 1) % peers) for i in range(1, peers, 2)]
    return near, lax.ppermute(value, LON, across + [(j, i) for i, j in across])


def passed_on(value):
    spots, halves = (lax.axis_size("x"), lax.axis_size("yh"))
    near = lax.ppermute(value, "yh", [(0, 1), (1, 0)])
    up = [(x * halves, (x + 1) * halves) for x in range(spots - 1)]
    down = [((x + 1) * halves + 1, x * halves + 1) for x in range(spots - 1)]
    return near, lax.ppermute(near, LAT, up + down)


def body(field, lat_kernel, lon_kernel, time_taps):
    rows_lat, rows_lon, length_in = field.shape
    steps_out = length_in - 2 * TH
    lat_place = lax.axis_index(LAT)
    total_lat = rows_lat * lax.axis_size(LAT)
    local = rows_lat * rows_lon
    cells = local * lax.axis_size(LAT) * lax.axis_size(LON)
    tall = -(-rows_lon // STEP) * STEP
    globrow = (lat_place * rows_lat + jnp.arange(rows_lat, dtype=jnp.int32)).astype(jnp.float32)
    latitude = jnp.pi * (globrow + 0.5) / total_lat - jnp.pi / 2
    weights = jnp.sqrt(jnp.cos(latitude))
    half = (local, TILE)
    lines = 4
    first, second = called(
        functools.partial(filter_kernel, lines),
        "filter",
        [half, half],
        [pltpu.VMEM, pltpu.HBM],
        [
            pltpu.VMEM((rows_lat, rows_lon, length_in), jnp.float32),
            pltpu.VMEM((rows_lat, tall, length_in), jnp.float32),
            pltpu.SemaphoreType.DMA((rows_lat // lines,)),
        ],
        time_taps[None],
        field,
        mib=56,
    )
    low = jnp.stack([lax.axis_index("yh") == 0, lax.axis_index("core") == 0]).astype(jnp.int32)
    bands = [(2 * SH, 6 * SH)] * 3
    lat_band, lon_band, lat_weighted = called(
        functools.partial(bands_kernel, SH),
        "bands",
        bands,
        [pltpu.SMEM] * 2,
        [],
        low,
        weights,
        lat_kernel[None],
        lon_kernel[None],
    )
    smooth = functools.partial(smooth_kernel, SH)
    near, far = passed_on(first)
    beside, beyond = around(second)
    (second,) = called(smooth, "lon", [half], [], [], lon_band, beside, second, beyond)
    (first,) = called(smooth, "lat", [half], [], [], lat_band, near, first, far)
    near, far = passed_on(second)
    beside, beyond = around(first)
    matrix, local_gram = called(
        functools.partial(last_kernel, SH),
        "last",
        [(2,) + half, (steps_out, steps_out)],
        [pltpu.SMEM],
        [],
        weights,
        lon_band,
        lat_weighted,
        beside,
        first,
        beyond,
        near,
        second,
        far,
    )
    gram = summed(local_gram)
    basis, merged = called(
        functools.partial(factor_kernel, cells),
        "factor",
        [(rows_lat, rows_lon, steps_out), (steps_out, steps_out)],
        [],
        [pltpu.VMEM((TILE, 2 * TILE), jnp.float32)],
        gram,
        matrix,
    )
    return (basis, merged)


def solution(mesh):
    fine = jax.sharding.Mesh(mesh.devices.reshape(4, 2, 2, 8, 2), ("x", "yh", "yl", "z", "core"))
    placed = (P(LAT, LON, None), P(), P(), P())
    return jax.shard_map(
        body, mesh=fine, in_specs=placed, out_specs=(P(LAT, LON, None), P()), check_vma=False
    )
```

```python
import functools

import jax
import jax.numpy as jnp
from jax import lax
from jax.experimental import pallas as pl
from jax.experimental.pallas import tpu as pltpu
from jax.sharding import PartitionSpec as P

TH = 64
SH = 20
LAT = ("x", "yh")
LON = ("yl", "z", "core")


PLANE = ("x", "yh", "yl")


def shared(value, axes):
    peers = lax.axis_size(axes)
    copies = jnp.broadcast_to(value[None], (peers,) + value.shape)
    return lax.all_to_all(copies, axes, 0, 0)


def summed(value):
    swap = [(0, 1), (1, 0)]
    core = lax.axis_index("core")
    rows, cols = value.shape
    half = rows // 2
    kept = lax.dynamic_slice_in_dim(value, core * half, half, 0)
    given = lax.dynamic_slice_in_dim(value, (1 - core) * half, half, 0)
    kept = kept + lax.ppermute(given, "core", swap)
    peers = lax.axis_size(PLANE)
    pieces = lax.all_to_all(kept.reshape(peers, half // peers, cols), PLANE, 0, 0)
    piece = shared(pieces.sum(axis=0), ("z",)).sum(axis=0)
    kept = shared(piece, PLANE).reshape(half, cols)
    given = lax.ppermute(kept, "core", swap)
    top = jnp.where(core == 0, kept, given)
    bottom = jnp.where(core == 0, given, kept)
    return jnp.concatenate([top, bottom], axis=0)


TILE = 128
STEP = 8

def product(left, right, over):
    return lax.dot_general(
        left,
        right,
        (over, ((), ())),
        precision=lax.Precision.HIGHEST,
        preferred_element_type=jnp.float32,
    )


def wide(value):
    return jnp.broadcast_to(value, (STEP, TILE))


def eliminate(work):
    for top in range(0, TILE, STEP):
        own = work[top:top + STEP, :TILE]
        cols = [wide(own[:, top + j:top + j + 1]) for j in range(STEP)]
        left = {(i, j): wide(cols[j][i:i + 1, :]) for j in range(STEP) for i in range(j + 1)}
        rows = [[wide(work[top + i:top + i + 1, s:s + TILE]) for s in (0, TILE)] for i in range(STEP)]
        root, upper = [], {}
        for j in range(STEP):
            root.append(lax.rsqrt(left[j, j]))
            for i in range(j + 1, STEP):
                upper[j, i] = left[j, i] * root[j]
            for i in range(j + 1, STEP):
                for n in range(i, STEP):
                    left[i, n] = left[i, n] - upper[j, i] * upper[j, n]
        for j in range(STEP):
            rows[j] = [value * root[j] for value in rows[j]]
            for i in range(j + 1, STEP):
                rows[i] = [value - upper[j, i] * done for value, done in zip(rows[i], rows[j])]
        for j in range(STEP):
            for half in range(2):
                work[top + j:top + j + 1, half * TILE:(half + 1) * TILE] = rows[j][half][:1, :]
        for below in range(top + STEP, TILE, STEP):
            parts = [work[below:below + STEP, s:s + TILE] for s in (0, TILE)]
            factors = [wide(parts[0][:, top + j:top + j + 1]) for j in range(STEP)]
            for j in range(STEP):
                factors[j] = factors[j] * root[j]
                for i in range(j + 1, STEP):
                    factors[i] = factors[i] - upper[j, i] * factors[j]
            for j in range(STEP):
                parts = [value - factors[j] * done for value, done in zip(parts, rows[j])]
            for half in range(2):
                work[below:below + STEP, half * TILE:(half + 1) * TILE] = parts[half]


ROWS = ((0,), (0,))
COLS = ((1,), (1,))
PLAIN = ((1,), (0,))


def factor_kernel(cells, gram, matrix, basis, merged, work):
    row = lax.broadcasted_iota(jnp.int32, (TILE, TILE), 0)
    col = lax.broadcasted_iota(jnp.int32, (TILE, TILE), 1)
    eye = jnp.where(row == col, 1.0, 0.0).astype(jnp.float32)
    scale = float(cells) ** 0.5

    def solve(block):
        work[:, :TILE] = block
        work[:, TILE:] = eye
        eliminate(work)
        upper = jnp.where(row <= col, work[:, :TILE], 0.0)
        lower = jnp.where(row >= col, work[:, TILE:], 0.0)
        return upper, lower

    r11, w11 = solve(gram[:TILE, :TILE])
    r12 = product(w11, gram[:TILE, TILE:], PLAIN)
    r22, w22 = solve(gram[TILE:, TILE:] - product(r12, r12, ROWS))
    w21 = -product(w22, product(r12, w11, ROWS), PLAIN)
    merged[:TILE, :TILE] = r11 * (1.0 / scale)
    merged[:TILE, TILE:] = r12 * (1.0 / scale)
    merged[TILE:, :TILE] = jnp.zeros((TILE, TILE), jnp.float32)
    merged[TILE:, TILE:] = r22 * (1.0 / scale)
    first, second = (matrix[0], matrix[1])
    left = product(first, w11 * scale, COLS)
    right = product(first, w21 * scale, COLS) + product(second, w22 * scale, COLS)
    lines, side, _ = basis.shape
    for line in range(lines):
        part = slice(line * side, (line + 1) * side)
        basis[line, :, :TILE] = left[part]
        basis[line, :, TILE:] = right[part]


def shifted(kernel, rows, start):
    flat = jnp.concatenate([kernel, jnp.zeros((1, TILE - kernel.shape[1]), jnp.float32)], axis=1)
    return pltpu.roll(jnp.broadcast_to(flat, (rows, TILE)), start, 1, stride=1, stride_axis=0)


def smoother(kernel, side):
    pair = 2 * side
    row = lax.broadcasted_iota(jnp.int32, (pair, TILE), 0)
    lane = lax.broadcasted_iota(jnp.int32, (pair, TILE), 1)
    total = jnp.zeros((pair, TILE), jnp.float32)
    for part in range(3):
        place = lane - part * pair
        inside = (place >= 0) & (place < pair) & ((place >= side) == (row >= side))
        total = jnp.where(inside, shifted(kernel, pair, part * side), total)
    return total[:, : 3 * pair]


def stacked(before, own, after, first, count):
    part = slice(first, first + count)
    return jnp.concatenate([lines[part, :] for lines in (before, own, after)], axis=0)


def turned(out, line, side, value):
    out[pl.ds(line, side, stride=out.shape[0] // side), :] = value


def ordered(first, kernel, side):
    pair = 2 * side
    plain = smoother(kernel[...], side)
    lead, middle, trail = (plain[:, at : at + pair] for at in (0, pair, 2 * pair))
    swapped = jnp.concatenate([trail, middle, lead], axis=1)
    return jnp.where(first == 1, swapped, plain)


def filter_kernel(low, weights, taps, lat_kernel, lon_kernel, field, first, second, lat_band, lon_band, lat_weighted, padded):
    rows, cols, hours = field.shape
    stride = padded.shape[1]
    count = taps.shape[1]
    lane = lax.broadcasted_iota(jnp.int32, (1, count), 1)
    full = taps[...] + jnp.where(lane == TH, 1.0, 0.0)
    full = jnp.concatenate([full, jnp.zeros((1, hours - count), jnp.float32)], axis=1)
    skew = pltpu.roll(jnp.broadcast_to(full, (2 * TILE, hours)), 0, 1, stride=1, stride_axis=0)
    padded[:, cols:, :] = jnp.zeros((rows, stride - cols, hours), jnp.float32)
    padded[:, :cols, :] = field[...]
    result = product(padded[...].reshape(rows * stride, hours), skew, COLS)
    for row in range(rows):
        value = result[row * stride : row * stride + cols]
        turned(first, row, cols, value[:, :TILE])
        second[row * cols : (row + 1) * cols, :] = value[:, TILE:]
    lat_band[...] = ordered(low[0], lat_kernel, SH)
    lon_band[...] = ordered(low[1], lon_kernel, SH)
    row = lax.broadcasted_iota(jnp.int32, (2 * SH, 1), 0)
    weight = jnp.zeros((2 * SH, 1), jnp.float32)
    for line in range(SH):
        weight = jnp.where((row == line) | (row == SH + line), weights[line], weight)
    lat_weighted[...] = lat_band[...] * weight


def smooth_kernel(side, band, near, own, far, out):
    pair = 2 * side
    for first in range(0, out.shape[0], pair):
        result = product(band[...], stacked(near, own, far, first, pair), PLAIN)
        for line in range(2):
            turned(out, first // side + line, side, result[line * side : (line + 1) * side])


def last_kernel(side, weights, lon_band, lat_band, *refs):
    parts, (out, gram) = (refs[:-2], refs[-2:])
    pair = 2 * side
    row = lax.broadcasted_iota(jnp.int32, (pair, 1), 0)
    for first in range(0, out.shape[1], pair):
        line = first // side
        weight = jnp.where(row < side, weights[line], weights[line + 1])
        result = product(lon_band[...], stacked(*parts[:3], first, pair), PLAIN)
        out[0, first : first + pair, :] = result * weight
        result = product(lat_band[...], stacked(*parts[3:], first, pair), PLAIN)
        for at in range(2):
            turned(out.at[1], line + at, side, result[at * side : (at + 1) * side])
    both = jnp.concatenate([out[0], out[1]], axis=1)
    gram[...] = product(both, both, ROWS)


def called(kernel, name, shapes, spaces, scratch, *args):
    spaces = list(spaces) + [pltpu.VMEM] * (len(args) - len(spaces))
    return pl.pallas_call(
        kernel,
        out_shape=[jax.ShapeDtypeStruct(shape, jnp.float32) for shape in shapes],
        in_specs=[pl.BlockSpec(memory_space=space) for space in spaces],
        out_specs=[pl.BlockSpec(memory_space=pltpu.VMEM)] * len(shapes),
        scratch_shapes=scratch,
        compiler_params=pltpu.CompilerParams(vmem_limit_bytes=24 * 1024 * 1024),
        name=name,
    )(*args)


def around(value):
    peers = lax.axis_size(LON)
    near = lax.ppermute(value, "core", [(0, 1), (1, 0)])
    across = [(i, (i + 1) % peers) for i in range(1, peers, 2)]
    return near, lax.ppermute(value, LON, across + [(j, i) for i, j in across])


def passed_on(value):
    spots, halves = (lax.axis_size("x"), lax.axis_size("yh"))
    near = lax.ppermute(value, "yh", [(0, 1), (1, 0)])
    up = [(x * halves, (x + 1) * halves) for x in range(spots - 1)]
    down = [((x + 1) * halves + 1, x * halves + 1) for x in range(spots - 1)]
    return near, lax.ppermute(near, LAT, up + down)


def body(field, lat_kernel, lon_kernel, time_taps):
    rows_lat, rows_lon, length_in = field.shape
    steps_out = length_in - 2 * TH
    lat_place = lax.axis_index(LAT)
    total_lat = rows_lat * lax.axis_size(LAT)
    local = rows_lat * rows_lon
    cells = local * lax.axis_size(LAT) * lax.axis_size(LON)
    tall = -(-rows_lon // STEP) * STEP
    globrow = (lat_place * rows_lat + jnp.arange(rows_lat, dtype=jnp.int32)).astype(jnp.float32)
    latitude = jnp.pi * (globrow + 0.5) / total_lat - jnp.pi / 2
    weights = jnp.sqrt(jnp.cos(latitude))
    half = (local, TILE)
    low = jnp.stack([lax.axis_index("yh") == 0, lax.axis_index("core") == 0]).astype(jnp.int32)
    first, second, lat_band, lon_band, lat_weighted = called(
        filter_kernel,
        "filter",
        [half, half] + [(2 * SH, 6 * SH)] * 3,
        [pltpu.SMEM] * 2,
        [pltpu.VMEM((rows_lat, tall, length_in), jnp.float32)],
        low,
        weights,
        time_taps[None],
        lat_kernel[None],
        lon_kernel[None],
        field,
    )
    smooth = functools.partial(smooth_kernel, SH)
    near, far = passed_on(first)
    beside, beyond = around(second)
    (second,) = called(smooth, "lon", [half], [], [], lon_band, beside, second, beyond)
    (first,) = called(smooth, "lat", [half], [], [], lat_band, near, first, far)
    near, far = passed_on(second)
    beside, beyond = around(first)
    matrix, local_gram = called(
        functools.partial(last_kernel, SH),
        "last",
        [(2,) + half, (steps_out, steps_out)],
        [pltpu.SMEM],
        [],
        weights,
        lon_band,
        lat_weighted,
        beside,
        first,
        beyond,
        near,
        second,
        far,
    )
    gram = summed(local_gram)
    basis, merged = called(
        functools.partial(factor_kernel, cells),
        "factor",
        [(rows_lat, rows_lon, steps_out), (steps_out, steps_out)],
        [],
        [pltpu.VMEM((TILE, 2 * TILE), jnp.float32)],
        gram,
        matrix,
    )
    return (basis, merged)


def solution(mesh):
    fine = jax.sharding.Mesh(mesh.devices.reshape(4, 2, 2, 8, 2), ("x", "yh", "yl", "z", "core"))
    placed = (P(LAT, LON, None), P(), P(), P())
    return jax.shard_map(
        body, mesh=fine, in_specs=placed, out_specs=(P(LAT, LON, None), P()), check_vma=False
    )
```

```python
import functools

import jax
import jax.numpy as jnp
from jax import lax
from jax.experimental import pallas as pl
from jax.experimental.pallas import tpu as pltpu
from jax.sharding import PartitionSpec as P

TH = 64
SH = 20
LAT = ("x", "yh")
LON = ("yl", "z", "core")


PLANE = ("x", "yh", "yl", "core")


def shared(value, axes):
    peers = lax.axis_size(axes)
    copies = jnp.broadcast_to(value[None], (peers,) + value.shape)
    return lax.all_to_all(copies, axes, 0, 0)


def summed(value):
    peers = lax.axis_size(PLANE)
    pieces = lax.all_to_all(value.reshape(peers, 1, value.size // peers), PLANE, 0, 0)
    piece = shared(pieces.sum(axis=0), ("z",)).sum(axis=0)
    return shared(piece, PLANE).reshape(value.shape)


TILE = 128
STEP = 8
PACK = TILE // 2

def product(left, right, over):
    return lax.dot_general(
        left,
        right,
        (over, ((), ())),
        precision=lax.Precision.HIGHEST,
        preferred_element_type=jnp.float32,
    )


def wide(value):
    return jnp.broadcast_to(value, (STEP, TILE))


def eliminate(work):
    for top in range(0, TILE, STEP):
        own = work[top:top + STEP, :TILE]
        cols = [wide(own[:, top + j:top + j + 1]) for j in range(STEP)]
        left = {(i, j): wide(cols[j][i:i + 1, :]) for j in range(STEP) for i in range(j + 1)}
        rows = [[wide(work[top + i:top + i + 1, s:s + TILE]) for s in (0, TILE)] for i in range(STEP)]
        root, upper = [], {}
        for j in range(STEP):
            root.append(lax.rsqrt(left[j, j]))
            for i in range(j + 1, STEP):
                upper[j, i] = left[j, i] * root[j]
            for i in range(j + 1, STEP):
                for n in range(i, STEP):
                    left[i, n] = left[i, n] - upper[j, i] * upper[j, n]
        for j in range(STEP):
            rows[j] = [value * root[j] for value in rows[j]]
            for i in range(j + 1, STEP):
                rows[i] = [value - upper[j, i] * done for value, done in zip(rows[i], rows[j])]
        for j in range(STEP):
            for half in range(2):
                work[top + j:top + j + 1, half * TILE:(half + 1) * TILE] = rows[j][half][:1, :]
        for below in range(top + STEP, TILE, STEP):
            parts = [work[below:below + STEP, s:s + TILE] for s in (0, TILE)]
            factors = [wide(parts[0][:, top + j:top + j + 1]) for j in range(STEP)]
            for j in range(STEP):
                factors[j] = factors[j] * root[j]
                for i in range(j + 1, STEP):
                    factors[i] = factors[i] - upper[j, i] * factors[j]
            for j in range(STEP):
                parts = [value - factors[j] * done for value, done in zip(parts, rows[j])]
            for half in range(2):
                work[below:below + STEP, half * TILE:(half + 1) * TILE] = parts[half]


ROWS = ((0,), (0,))
COLS = ((1,), (1,))
PLAIN = ((1,), (0,))


def factor_kernel(cells, gram, matrix, basis, merged, work):
    row = lax.broadcasted_iota(jnp.int32, (TILE, TILE), 0)
    col = lax.broadcasted_iota(jnp.int32, (TILE, TILE), 1)
    eye = jnp.where(row == col, 1.0, 0.0).astype(jnp.float32)
    scale = float(cells) ** 0.5

    def solve(block):
        work[:, :TILE] = block
        work[:, TILE:] = eye
        eliminate(work)
        upper = jnp.where(row <= col, work[:, :TILE], 0.0)
        lower = jnp.where(row >= col, work[:, TILE:], 0.0)
        return upper, lower

    blocks = [gram[at * PACK : (at + 1) * PACK, :] for at in range(5)]
    r11, w11 = solve(mirrored(blocks[0], blocks[4]))
    r12 = product(w11, jnp.concatenate(blocks[1:3], axis=0), PLAIN)
    a22 = mirrored(blocks[3], pltpu.roll(blocks[4], PACK, 1))
    r22, w22 = solve(a22 - product(r12, r12, ROWS))
    w21 = -product(w22, product(r12, w11, ROWS), PLAIN)
    merged[:TILE, :TILE] = r11 * (1.0 / scale)
    merged[:TILE, TILE:] = r12 * (1.0 / scale)
    merged[TILE:, :TILE] = jnp.zeros((TILE, TILE), jnp.float32)
    merged[TILE:, TILE:] = r22 * (1.0 / scale)
    first, second = (matrix[0], matrix[1])
    left = product(first, w11 * scale, COLS)
    right = product(first, w21 * scale, COLS) + product(second, w22 * scale, COLS)
    lines, side, _ = basis.shape
    for line in range(lines):
        part = slice(line * side, (line + 1) * side)
        basis[line, :, :TILE] = left[part]
        basis[line, :, TILE:] = right[part]


def shifted(kernel, rows, start):
    flat = jnp.concatenate([kernel, jnp.zeros((1, TILE - kernel.shape[1]), jnp.float32)], axis=1)
    return pltpu.roll(jnp.broadcast_to(flat, (rows, TILE)), start, 1, stride=1, stride_axis=0)


def smoother(kernel, side):
    pair = 2 * side
    row = lax.broadcasted_iota(jnp.int32, (pair, TILE), 0)
    lane = lax.broadcasted_iota(jnp.int32, (pair, TILE), 1)
    total = jnp.zeros((pair, TILE), jnp.float32)
    for part in range(3):
        place = lane - part * pair
        inside = (place >= 0) & (place < pair) & ((place >= side) == (row >= side))
        total = jnp.where(inside, shifted(kernel, pair, part * side), total)
    return total[:, : 3 * pair]


def stacked(before, own, after, first, count):
    part = slice(first, first + count)
    return jnp.concatenate([lines[part, :] for lines in (before, own, after)], axis=0)


def turned(out, line, side, value):
    out[pl.ds(line, side, stride=out.shape[0] // side), :] = value


def ordered(first, kernel, side):
    pair = 2 * side
    plain = smoother(kernel[...], side)
    lead, middle, trail = (plain[:, at : at + pair] for at in (0, pair, 2 * pair))
    swapped = jnp.concatenate([trail, middle, lead], axis=1)
    return jnp.where(first == 1, swapped, plain)


def filtered(taps, field, padded, start):
    rows, cols, hours = padded.shape
    side = field.shape[1]
    count = taps.shape[1]
    lane = lax.broadcasted_iota(jnp.int32, (1, count), 1)
    full = taps[...] + jnp.where(lane == TH, 1.0, 0.0)
    full = jnp.concatenate([full, jnp.zeros((1, hours - count), jnp.float32)], axis=1)
    skew = pltpu.roll(jnp.broadcast_to(full, (TILE, hours)), 0, 1, stride=1, stride_axis=0)
    padded[:, side:, :] = jnp.zeros((rows, cols - side, hours), jnp.float32)
    padded[:, :side, :] = field[:, :, start : start + hours]
    return product(padded[...].reshape(rows * cols, hours), skew, COLS)


def early_kernel(taps, field, out, padded):
    rows, side, _ = field.shape
    result = filtered(taps, field, padded, 0)
    for row in range(rows):
        at = row * padded.shape[1]
        turned(out, row, side, result[at : at + side])


def late_kernel(low, weights, taps, lat_kernel, lon_kernel, field, out, lat_band, lon_band, lat_weighted, padded):
    rows, side, _ = field.shape
    result = filtered(taps, field, padded, TILE)
    for row in range(rows):
        at = row * padded.shape[1]
        out[row * side : (row + 1) * side, :] = result[at : at + side]
    lat_band[...] = ordered(low[0], lat_kernel, SH)
    lon_band[...] = ordered(low[1], lon_kernel, SH)
    row = lax.broadcasted_iota(jnp.int32, (2 * SH, 1), 0)
    weight = jnp.zeros((2 * SH, 1), jnp.float32)
    for line in range(SH):
        weight = jnp.where((row == line) | (row == SH + line), weights[line], weight)
    lat_weighted[...] = lat_band[...] * weight


def smooth_kernel(side, band, near, own, far, out):
    pair = 2 * side
    for first in range(0, out.shape[0], pair):
        result = product(band[...], stacked(near, own, far, first, pair), PLAIN)
        for line in range(2):
            turned(out, first // side + line, side, result[line * side : (line + 1) * side])


def packed_corner(first, second):
    lane = lax.broadcasted_iota(jnp.int32, (PACK, TILE), 1)
    return jnp.where(lane < PACK, pltpu.roll(second[PACK:], PACK, 1), first[PACK:])


def mirrored(top, corner):
    row = lax.broadcasted_iota(jnp.int32, (TILE, TILE), 0)
    lane = lax.broadcasted_iota(jnp.int32, (TILE, TILE), 1)
    upper = jnp.concatenate([top, corner], axis=0)
    return jnp.where((row >= PACK) & (lane < PACK), upper.T, upper)


def last_kernel(side, weights, lon_band, lat_band, *refs):
    parts, (out, gram) = (refs[:-2], refs[-2:])
    pair = 2 * side
    row = lax.broadcasted_iota(jnp.int32, (pair, 1), 0)
    for first in range(0, out.shape[1], pair):
        line = first // side
        weight = jnp.where(row < side, weights[line], weights[line + 1])
        result = product(lon_band[...], stacked(*parts[:3], first, pair), PLAIN)
        out[0, first : first + pair, :] = result * weight
        result = product(lat_band[...], stacked(*parts[3:], first, pair), PLAIN)
        for at in range(2):
            turned(out.at[1], line + at, side, result[at * side : (at + 1) * side])
    early, late = (out[0], out[1])
    first = product(early, early, ROWS)
    cross = product(early, late, ROWS)
    second = product(late, late, ROWS)
    packed = packed_corner(first, second)
    for at, block in enumerate((first[:PACK], cross[:PACK], cross[PACK:], second[:PACK], packed)):
        gram[at * PACK : (at + 1) * PACK, :] = block


def called(kernel, name, shapes, spaces, scratch, *args):
    spaces = list(spaces) + [pltpu.VMEM] * (len(args) - len(spaces))
    return pl.pallas_call(
        kernel,
        out_shape=[jax.ShapeDtypeStruct(shape, jnp.float32) for shape in shapes],
        in_specs=[pl.BlockSpec(memory_space=space) for space in spaces],
        out_specs=[pl.BlockSpec(memory_space=pltpu.VMEM)] * len(shapes),
        scratch_shapes=scratch,
        compiler_params=pltpu.CompilerParams(vmem_limit_bytes=24 * 1024 * 1024),
        name=name,
    )(*args)


def around(value):
    peers = lax.axis_size(LON)
    near = lax.ppermute(value, "core", [(0, 1), (1, 0)])
    across = [(i, (i + 1) % peers) for i in range(1, peers, 2)]
    return near, lax.ppermute(value, LON, across + [(j, i) for i, j in across])


def passed_on(value):
    spots, halves = (lax.axis_size("x"), lax.axis_size("yh"))
    near = lax.ppermute(value, "yh", [(0, 1), (1, 0)])
    up = [(x * halves, (x + 1) * halves) for x in range(spots - 1)]
    down = [((x + 1) * halves + 1, x * halves + 1) for x in range(spots - 1)]
    return near, lax.ppermute(near, LAT, up + down)


def body(field, lat_kernel, lon_kernel, time_taps):
    rows_lat, rows_lon, length_in = field.shape
    steps_out = length_in - 2 * TH
    lat_place = lax.axis_index(LAT)
    total_lat = rows_lat * lax.axis_size(LAT)
    local = rows_lat * rows_lon
    cells = local * lax.axis_size(LAT) * lax.axis_size(LON)
    tall = -(-rows_lon // STEP) * STEP
    globrow = (lat_place * rows_lat + jnp.arange(rows_lat, dtype=jnp.int32)).astype(jnp.float32)
    latitude = jnp.pi * (globrow + 0.5) / total_lat - jnp.pi / 2
    weights = jnp.sqrt(jnp.cos(latitude))
    half = (local, TILE)
    low = jnp.stack([lax.axis_index("yh") == 0, lax.axis_index("core") == 0]).astype(jnp.int32)
    padded = [pltpu.VMEM((rows_lat, tall, 2 * TILE), jnp.float32)]
    (first,) = called(early_kernel, "early", [half], [], padded, time_taps[None], field)
    second, lat_band, lon_band, lat_weighted = called(
        late_kernel,
        "late",
        [half] + [(2 * SH, 6 * SH)] * 3,
        [pltpu.SMEM] * 2,
        padded,
        low,
        weights,
        time_taps[None],
        lat_kernel[None],
        lon_kernel[None],
        field,
    )
    smooth = functools.partial(smooth_kernel, SH)
    near, far = passed_on(first)
    beside, beyond = around(second)
    (second,) = called(smooth, "lon", [half], [], [], lon_band, beside, second, beyond)
    (first,) = called(smooth, "lat", [half], [], [], lat_band, near, first, far)
    near, far = passed_on(second)
    beside, beyond = around(first)
    matrix, local_gram = called(
        functools.partial(last_kernel, SH),
        "last",
        [(2,) + half, (5 * PACK, TILE)],
        [pltpu.SMEM],
        [],
        weights,
        lon_band,
        lat_weighted,
        beside,
        first,
        beyond,
        near,
        second,
        far,
    )
    gram = summed(local_gram)
    basis, merged = called(
        functools.partial(factor_kernel, cells),
        "factor",
        [(rows_lat, rows_lon, steps_out), (steps_out, steps_out)],
        [],
        [pltpu.VMEM((TILE, 2 * TILE), jnp.float32)],
        gram,
        matrix,
    )
    return (basis, merged)


def solution(mesh):
    fine = jax.sharding.Mesh(mesh.devices.reshape(4, 2, 2, 8, 2), ("x", "yh", "yl", "z", "core"))
    placed = (P(LAT, LON, None), P(), P(), P())
    return jax.shard_map(
        body, mesh=fine, in_specs=placed, out_specs=(P(LAT, LON, None), P()), check_vma=False
    )
```

```python
import functools

import jax
import jax.numpy as jnp
from jax import lax
from jax.experimental import pallas as pl
from jax.experimental.pallas import tpu as pltpu
from jax.sharding import PartitionSpec as P

TH = 64
SH = 20
LAT = ("x", "yh")
LON = ("yl", "z", "core")


PLANE = ("x", "yh", "yl", "core")


def shared(value, axes):
    peers = lax.axis_size(axes)
    copies = jnp.broadcast_to(value[None], (peers,) + value.shape)
    return lax.all_to_all(copies, axes, 0, 0)


def summed(value):
    peers = lax.axis_size(PLANE)
    pieces = lax.all_to_all(value.reshape(peers, 1, value.size // peers), PLANE, 0, 0)
    piece = shared(pieces.sum(axis=0), ("z",)).sum(axis=0)
    return shared(piece, PLANE).reshape(value.shape)


TILE = 128
STEP = 8
PACK = TILE // 2

def product(left, right, over):
    return lax.dot_general(
        left,
        right,
        (over, ((), ())),
        precision=lax.Precision.HIGHEST,
        preferred_element_type=jnp.float32,
    )


def wide(value):
    return jnp.broadcast_to(value, (STEP, TILE))


def eliminate(work):
    for top in range(0, TILE, STEP):
        flat = [wide(work[top + i:top + i + 1, :TILE]) for i in range(STEP)]
        left = {(i, j): wide(flat[i][:, top + j:top + j + 1]) for j in range(STEP) for i in range(j + 1)}
        rows = [[wide(work[top + i:top + i + 1, s:s + TILE]) for s in (0, TILE)] for i in range(STEP)]
        root, upper = [], {}
        for j in range(STEP):
            root.append(lax.rsqrt(left[j, j]))
            for i in range(j + 1, STEP):
                upper[j, i] = left[j, i] * root[j]
            for i in range(j + 1, STEP):
                for n in range(i, STEP):
                    left[i, n] = left[i, n] - upper[j, i] * upper[j, n]
        for j in range(STEP):
            rows[j] = [value * root[j] for value in rows[j]]
            for i in range(j + 1, STEP):
                rows[i] = [value - upper[j, i] * done for value, done in zip(rows[i], rows[j])]
        for j in range(STEP):
            for half in range(2):
                work[top + j:top + j + 1, half * TILE:(half + 1) * TILE] = rows[j][half][:1, :]
        for below in range(top + STEP, TILE, STEP):
            parts = [work[below:below + STEP, s:s + TILE] for s in (0, TILE)]
            factors = [wide(parts[0][:, top + j:top + j + 1]) for j in range(STEP)]
            for j in range(STEP):
                factors[j] = factors[j] * root[j]
                for i in range(j + 1, STEP):
                    factors[i] = factors[i] - upper[j, i] * factors[j]
            for half in range(2):
                terms = [factors[j] * rows[j][half] for j in range(STEP)]
                while len(terms) > 1:
                    terms = [one + other for one, other in zip(terms[::2], terms[1::2])]
                parts[half] = parts[half] - terms[0]
            for half in range(2):
                work[below:below + STEP, half * TILE:(half + 1) * TILE] = parts[half]


ROWS = ((0,), (0,))
COLS = ((1,), (1,))
PLAIN = ((1,), (0,))


def factor_kernel(cells, gram, matrix, basis, merged, work):
    row = lax.broadcasted_iota(jnp.int32, (TILE, TILE), 0)
    col = lax.broadcasted_iota(jnp.int32, (TILE, TILE), 1)
    eye = jnp.where(row == col, 1.0, 0.0).astype(jnp.float32)
    scale = float(cells) ** 0.5

    def solve(block):
        work[:, :TILE] = block
        work[:, TILE:] = eye
        eliminate(work)
        upper = jnp.where(row <= col, work[:, :TILE], 0.0)
        lower = jnp.where(row >= col, work[:, TILE:], 0.0)
        return upper, lower

    blocks = [gram[at * PACK : (at + 1) * PACK, :] for at in range(5)]
    r11, w11 = solve(mirrored(blocks[0], blocks[4]))
    r12 = product(w11, jnp.concatenate(blocks[1:3], axis=0), PLAIN)
    a22 = mirrored(blocks[3], pltpu.roll(blocks[4], PACK, 1)) - product(r12, r12, ROWS)
    left = product(matrix[0], w11, COLS)
    rest = matrix[1] - product(left, r12, PLAIN)
    r22, w22 = solve(a22)
    right = product(rest, w22 * scale, COLS)
    merged[:TILE, :TILE] = r11 * (1.0 / scale)
    merged[:TILE, TILE:] = r12 * (1.0 / scale)
    merged[TILE:, :TILE] = jnp.zeros((TILE, TILE), jnp.float32)
    merged[TILE:, TILE:] = r22 * (1.0 / scale)
    lines, side, _ = basis.shape
    for line in range(lines):
        part = slice(line * side, (line + 1) * side)
        basis[line, :, :TILE] = left[part] * scale
        basis[line, :, TILE:] = right[part]


def shifted(kernel, rows, start):
    flat = jnp.concatenate([kernel, jnp.zeros((1, TILE - kernel.shape[1]), jnp.float32)], axis=1)
    return pltpu.roll(jnp.broadcast_to(flat, (rows, TILE)), start, 1, stride=1, stride_axis=0)


def smoother(kernel, side):
    pair = 2 * side
    row = lax.broadcasted_iota(jnp.int32, (pair, TILE), 0)
    lane = lax.broadcasted_iota(jnp.int32, (pair, TILE), 1)
    total = jnp.zeros((pair, TILE), jnp.float32)
    for part in range(3):
        place = lane - part * pair
        inside = (place >= 0) & (place < pair) & ((place >= side) == (row >= side))
        total = jnp.where(inside, shifted(kernel, pair, part * side), total)
    return total[:, : 3 * pair]


def stacked(before, own, after, first, count):
    part = slice(first, first + count)
    return jnp.concatenate([lines[part, :] for lines in (before, own, after)], axis=0)


def turned(out, line, side, value):
    out[pl.ds(line, side, stride=out.shape[0] // side), :] = value


def ordered(first, kernel, side):
    pair = 2 * side
    plain = smoother(kernel[...], side)
    lead, middle, trail = (plain[:, at : at + pair] for at in (0, pair, 2 * pair))
    swapped = jnp.concatenate([trail, middle, lead], axis=1)
    return jnp.where(first == 1, swapped, plain)


def filtered(taps, field, padded, start):
    rows, cols, hours = padded.shape
    side = field.shape[1]
    count = taps.shape[1]
    lane = lax.broadcasted_iota(jnp.int32, (1, count), 1)
    full = taps[...] + jnp.where(lane == TH, 1.0, 0.0)
    full = jnp.concatenate([full, jnp.zeros((1, hours - count), jnp.float32)], axis=1)
    skew = pltpu.roll(jnp.broadcast_to(full, (TILE, hours)), 0, 1, stride=1, stride_axis=0)
    padded[:, side:, :] = jnp.zeros((rows, cols - side, hours), jnp.float32)
    padded[:, :side, :] = field[:, :, start : start + hours]
    return product(padded[...].reshape(rows * cols, hours), skew, COLS)


def early_kernel(taps, field, out, padded):
    rows, side, _ = field.shape
    result = filtered(taps, field, padded, 0)
    for row in range(rows):
        at = row * padded.shape[1]
        turned(out, row, side, result[at : at + side])


def late_kernel(low, weights, taps, lat_kernel, lon_kernel, field, out, lat_band, lon_band, lat_weighted, padded):
    rows, side, _ = field.shape
    result = filtered(taps, field, padded, TILE)
    for row in range(rows):
        at = row * padded.shape[1]
        out[row * side : (row + 1) * side, :] = result[at : at + side]
    lat_band[...] = ordered(low[0], lat_kernel, SH)
    lon_band[...] = ordered(low[1], lon_kernel, SH)
    row = lax.broadcasted_iota(jnp.int32, (2 * SH, 1), 0)
    weight = jnp.zeros((2 * SH, 1), jnp.float32)
    for line in range(SH):
        weight = jnp.where((row == line) | (row == SH + line), weights[line], weight)
    lat_weighted[...] = lat_band[...] * weight


def smooth_kernel(side, band, near, own, far, out):
    pair = 2 * side
    for first in range(0, out.shape[0], pair):
        result = product(band[...], stacked(near, own, far, first, pair), PLAIN)
        for line in range(2):
            turned(out, first // side + line, side, result[line * side : (line + 1) * side])


def packed_corner(first, second):
    lane = lax.broadcasted_iota(jnp.int32, (PACK, TILE), 1)
    return jnp.where(lane < PACK, pltpu.roll(second[PACK:], PACK, 1), first[PACK:])


def mirrored(top, corner):
    row = lax.broadcasted_iota(jnp.int32, (TILE, TILE), 0)
    lane = lax.broadcasted_iota(jnp.int32, (TILE, TILE), 1)
    upper = jnp.concatenate([top, corner], axis=0)
    return jnp.where((row >= PACK) & (lane < PACK), upper.T, upper)


def last_kernel(side, weights, lon_band, lat_band, *refs):
    parts, (out, gram) = (refs[:-2], refs[-2:])
    pair = 2 * side
    row = lax.broadcasted_iota(jnp.int32, (pair, 1), 0)
    for first in range(0, out.shape[1], pair):
        line = first // side
        weight = jnp.where(row < side, weights[line], weights[line + 1])
        result = product(lon_band[...], stacked(*parts[:3], first, pair), PLAIN)
        out[0, first : first + pair, :] = result * weight
        result = product(lat_band[...], stacked(*parts[3:], first, pair), PLAIN)
        for at in range(2):
            turned(out.at[1], line + at, side, result[at * side : (at + 1) * side])
    early, late = (out[0], out[1])
    first = product(early, early, ROWS)
    cross = product(early, late, ROWS)
    second = product(late, late, ROWS)
    packed = packed_corner(first, second)
    for at, block in enumerate((first[:PACK], cross[:PACK], cross[PACK:], second[:PACK], packed)):
        gram[at * PACK : (at + 1) * PACK, :] = block


def called(kernel, name, shapes, spaces, scratch, *args):
    spaces = list(spaces) + [pltpu.VMEM] * (len(args) - len(spaces))
    return pl.pallas_call(
        kernel,
        out_shape=[jax.ShapeDtypeStruct(shape, jnp.float32) for shape in shapes],
        in_specs=[pl.BlockSpec(memory_space=space) for space in spaces],
        out_specs=[pl.BlockSpec(memory_space=pltpu.VMEM)] * len(shapes),
        scratch_shapes=scratch,
        compiler_params=pltpu.CompilerParams(vmem_limit_bytes=24 * 1024 * 1024),
        name=name,
    )(*args)


def around(value):
    peers = lax.axis_size(LON)
    near = lax.ppermute(value, "core", [(0, 1), (1, 0)])
    across = [(i, (i + 1) % peers) for i in range(1, peers, 2)]
    return near, lax.ppermute(value, LON, across + [(j, i) for i, j in across])


def passed_on(value):
    spots, halves = (lax.axis_size("x"), lax.axis_size("yh"))
    near = lax.ppermute(value, "yh", [(0, 1), (1, 0)])
    up = [(x * halves, (x + 1) * halves) for x in range(spots - 1)]
    down = [((x + 1) * halves + 1, x * halves + 1) for x in range(spots - 1)]
    return near, lax.ppermute(near, LAT, up + down)


def body(field, lat_kernel, lon_kernel, time_taps):
    rows_lat, rows_lon, length_in = field.shape
    steps_out = length_in - 2 * TH
    lat_place = lax.axis_index(LAT)
    total_lat = rows_lat * lax.axis_size(LAT)
    local = rows_lat * rows_lon
    cells = local * lax.axis_size(LAT) * lax.axis_size(LON)
    tall = -(-rows_lon // STEP) * STEP
    globrow = (lat_place * rows_lat + jnp.arange(rows_lat, dtype=jnp.int32)).astype(jnp.float32)
    latitude = jnp.pi * (globrow + 0.5) / total_lat - jnp.pi / 2
    weights = jnp.sqrt(jnp.cos(latitude))
    half = (local, TILE)
    low = jnp.stack([lax.axis_index("yh") == 0, lax.axis_index("core") == 0]).astype(jnp.int32)
    padded = [pltpu.VMEM((rows_lat, tall, 2 * TILE), jnp.float32)]
    (first,) = called(early_kernel, "early", [half], [], padded, time_taps[None], field)
    second, lat_band, lon_band, lat_weighted = called(
        late_kernel,
        "late",
        [half] + [(2 * SH, 6 * SH)] * 3,
        [pltpu.SMEM] * 2,
        padded,
        low,
        weights,
        time_taps[None],
        lat_kernel[None],
        lon_kernel[None],
        field,
    )
    smooth = functools.partial(smooth_kernel, SH)
    near, far = passed_on(first)
    beside, beyond = around(second)
    (second,) = called(smooth, "lon", [half], [], [], lon_band, beside, second, beyond)
    (first,) = called(smooth, "lat", [half], [], [], lat_band, near, first, far)
    near, far = passed_on(second)
    beside, beyond = around(first)
    matrix, local_gram = called(
        functools.partial(last_kernel, SH),
        "last",
        [(2,) + half, (5 * PACK, TILE)],
        [pltpu.SMEM],
        [],
        weights,
        lon_band,
        lat_weighted,
        beside,
        first,
        beyond,
        near,
        second,
        far,
    )
    gram = summed(local_gram)
    basis, merged = called(
        functools.partial(factor_kernel, cells),
        "factor",
        [(rows_lat, rows_lon, steps_out), (steps_out, steps_out)],
        [],
        [pltpu.VMEM((TILE, 2 * TILE), jnp.float32)],
        gram,
        matrix,
    )
    return (basis, merged)


def solution(mesh):
    fine = jax.sharding.Mesh(mesh.devices.reshape(4, 2, 2, 8, 2), ("x", "yh", "yl", "z", "core"))
    placed = (P(LAT, LON, None), P(), P(), P())
    return jax.shard_map(
        body, mesh=fine, in_specs=placed, out_specs=(P(LAT, LON, None), P()), check_vma=False
    )
```

```python
import functools

import jax
import jax.numpy as jnp
from jax import lax
from jax.experimental import pallas as pl
from jax.experimental.pallas import tpu as pltpu
from jax.sharding import PartitionSpec as P

TH = 64
SH = 20
LAT = ("x", "yh")
LON = ("yl", "z", "core")


PLANE = ("x", "yh", "yl", "core")


def shared(value, axes):
    peers = lax.axis_size(axes)
    copies = jnp.broadcast_to(value[None], (peers,) + value.shape)
    return lax.all_to_all(copies, axes, 0, 0)


def summed(value):
    peers = lax.axis_size(PLANE)
    pieces = lax.all_to_all(value.reshape(peers, 1, value.size // peers), PLANE, 0, 0)
    piece = shared(pieces.sum(axis=0), ("z",)).sum(axis=0)
    return shared(piece, PLANE).reshape(value.shape)


TILE = 128
STEP = 8
PACK = TILE // 2

def product(left, right, over):
    return lax.dot_general(
        left,
        right,
        (over, ((), ())),
        precision=lax.Precision.HIGHEST,
        preferred_element_type=jnp.float32,
    )


def wide(value):
    return jnp.broadcast_to(value, (STEP, TILE))


def eliminate(work):
    for top in range(0, TILE, STEP):
        flat = [wide(work[top + i:top + i + 1, :TILE]) for i in range(STEP)]
        left = {(i, j): wide(flat[i][:, top + j:top + j + 1]) for j in range(STEP) for i in range(j + 1)}
        rows = [[wide(work[top + i:top + i + 1, s:s + TILE]) for s in (0, TILE)] for i in range(STEP)]
        root, upper = [], {}
        for j in range(STEP):
            root.append(lax.rsqrt(left[j, j]))
            for i in range(j + 1, STEP):
                upper[j, i] = left[j, i] * root[j]
            for i in range(j + 1, STEP):
                for n in range(i, STEP):
                    left[i, n] = left[i, n] - upper[j, i] * upper[j, n]
        for j in range(STEP):
            rows[j] = [value * root[j] for value in rows[j]]
            for i in range(j + 1, STEP):
                rows[i] = [value - upper[j, i] * done for value, done in zip(rows[i], rows[j])]
        for j in range(STEP):
            for half in range(2):
                work[top + j:top + j + 1, half * TILE:(half + 1) * TILE] = rows[j][half][:1, :]
        for below in range(top + STEP, TILE, STEP):
            parts = [work[below:below + STEP, s:s + TILE] for s in (0, TILE)]
            factors = [wide(parts[0][:, top + j:top + j + 1]) for j in range(STEP)]
            for j in range(STEP):
                factors[j] = factors[j] * root[j]
                for i in range(j + 1, STEP):
                    factors[i] = factors[i] - upper[j, i] * factors[j]
            for half in range(2):
                terms = [factors[j] * rows[j][half] for j in range(STEP)]
                while len(terms) > 1:
                    terms = [one + other for one, other in zip(terms[::2], terms[1::2])]
                parts[half] = parts[half] - terms[0]
            for half in range(2):
                work[below:below + STEP, half * TILE:(half + 1) * TILE] = parts[half]


ROWS = ((0,), (0,))
COLS = ((1,), (1,))
PLAIN = ((1,), (0,))


def factor_kernel(cells, gram, matrix, basis, merged, work):
    row = lax.broadcasted_iota(jnp.int32, (TILE, TILE), 0)
    col = lax.broadcasted_iota(jnp.int32, (TILE, TILE), 1)
    eye = jnp.where(row == col, 1.0, 0.0).astype(jnp.float32)
    scale = float(cells) ** 0.5

    def solve(block):
        work[:, :TILE] = block
        work[:, TILE:] = eye
        eliminate(work)
        upper = jnp.where(row <= col, work[:, :TILE], 0.0)
        lower = jnp.where(row >= col, work[:, TILE:], 0.0)
        return upper, lower

    blocks = [gram[at * PACK : (at + 1) * PACK, :] for at in range(5)]
    r11, w11 = solve(mirrored(blocks[0], blocks[4]))
    r12 = product(w11, jnp.concatenate(blocks[1:3], axis=0), PLAIN)
    a22 = mirrored(blocks[3], pltpu.roll(blocks[4], PACK, 1)) - product(r12, r12, ROWS)
    left = product(matrix[0], w11, COLS)
    rest = matrix[1] - product(left, r12, PLAIN)
    r22, w22 = solve(a22)
    right = product(rest, w22 * scale, COLS)
    merged[:TILE, :TILE] = r11 * (1.0 / scale)
    merged[:TILE, TILE:] = r12 * (1.0 / scale)
    merged[TILE:, :TILE] = jnp.zeros((TILE, TILE), jnp.float32)
    merged[TILE:, TILE:] = r22 * (1.0 / scale)
    lines, side, _ = basis.shape
    for line in range(lines):
        part = slice(line * side, (line + 1) * side)
        basis[line, :, :TILE] = left[part] * scale
        basis[line, :, TILE:] = right[part]


def shifted(kernel, rows, start):
    flat = jnp.concatenate([kernel, jnp.zeros((1, TILE - kernel.shape[1]), jnp.float32)], axis=1)
    return pltpu.roll(jnp.broadcast_to(flat, (rows, TILE)), start, 1, stride=1, stride_axis=0)


def smoother(kernel, side):
    pair = 2 * side
    row = lax.broadcasted_iota(jnp.int32, (pair, TILE), 0)
    lane = lax.broadcasted_iota(jnp.int32, (pair, TILE), 1)
    total = jnp.zeros((pair, TILE), jnp.float32)
    for part in range(3):
        place = lane - part * pair
        inside = (place >= 0) & (place < pair) & ((place >= side) == (row >= side))
        total = jnp.where(inside, shifted(kernel, pair, part * side), total)
    return total[:, : 3 * pair]


def stacked(before, own, after, first, count):
    part = slice(first, first + count)
    return jnp.concatenate([lines[part, :] for lines in (before, own, after)], axis=0)


def turned(out, line, side, value):
    out[pl.ds(line, side, stride=out.shape[0] // side), :] = value


def ordered(first, kernel, side):
    pair = 2 * side
    plain = smoother(kernel[...], side)
    lead, middle, trail = (plain[:, at : at + pair] for at in (0, pair, 2 * pair))
    swapped = jnp.concatenate([trail, middle, lead], axis=1)
    return jnp.where(first == 1, swapped, plain)


def filtered(taps, field, padded, start):
    rows, cols, hours = padded.shape
    side = field.shape[1]
    count = taps.shape[1]
    lane = lax.broadcasted_iota(jnp.int32, (1, count), 1)
    full = taps[...] + jnp.where(lane == TH, 1.0, 0.0)
    full = jnp.concatenate([full, jnp.zeros((1, hours - count), jnp.float32)], axis=1)
    skew = pltpu.roll(jnp.broadcast_to(full, (TILE, hours)), 0, 1, stride=1, stride_axis=0)
    padded[:, side:, :] = jnp.zeros((rows, cols - side, hours), jnp.float32)
    padded[:, :side, :] = field[:, :, start : start + hours]
    return product(padded[...].reshape(rows * cols, hours), skew, COLS)


def early_kernel(taps, lat_kernel, lon_kernel, field, out, lat_out, lon_out, padded):
    lat_out[...] = lat_kernel[...]
    lon_out[...] = lon_kernel[...]
    rows, side, _ = field.shape
    result = filtered(taps, field, padded, 0)
    for row in range(rows):
        at = row * padded.shape[1]
        turned(out, row, side, result[at : at + side])


def late_kernel(low, weights, taps, lat_kernel, lon_kernel, field, out, lat_band, lon_band, lat_weighted, padded):
    rows, side, _ = field.shape
    result = filtered(taps, field, padded, TILE)
    for row in range(rows):
        at = row * padded.shape[1]
        out[row * side : (row + 1) * side, :] = result[at : at + side]
    lat_band[...] = ordered(low[0], lat_kernel, SH)
    lon_band[...] = ordered(low[1], lon_kernel, SH)
    row = lax.broadcasted_iota(jnp.int32, (2 * SH, 1), 0)
    weight = jnp.zeros((2 * SH, 1), jnp.float32)
    for line in range(SH):
        weight = jnp.where((row == line) | (row == SH + line), weights[line], weight)
    lat_weighted[...] = lat_band[...] * weight


def smooth_kernel(side, band, near, own, far, out):
    pair = 2 * side
    for first in range(0, out.shape[0], pair):
        result = product(band[...], stacked(near, own, far, first, pair), PLAIN)
        for line in range(2):
            turned(out, first // side + line, side, result[line * side : (line + 1) * side])


def packed_corner(first, second):
    lane = lax.broadcasted_iota(jnp.int32, (PACK, TILE), 1)
    return jnp.where(lane < PACK, pltpu.roll(second[PACK:], PACK, 1), first[PACK:])


def mirrored(top, corner):
    row = lax.broadcasted_iota(jnp.int32, (TILE, TILE), 0)
    lane = lax.broadcasted_iota(jnp.int32, (TILE, TILE), 1)
    upper = jnp.concatenate([top, corner], axis=0)
    return jnp.where((row >= PACK) & (lane < PACK), upper.T, upper)


def last_kernel(side, weights, lon_band, lat_band, *refs):
    parts, (out, gram) = (refs[:-2], refs[-2:])
    pair = 2 * side
    row = lax.broadcasted_iota(jnp.int32, (pair, 1), 0)
    for first in range(0, out.shape[1], pair):
        line = first // side
        weight = jnp.where(row < side, weights[line], weights[line + 1])
        result = product(lon_band[...], stacked(*parts[:3], first, pair), PLAIN)
        out[0, first : first + pair, :] = result * weight
        result = product(lat_band[...], stacked(*parts[3:], first, pair), PLAIN)
        for at in range(2):
            turned(out.at[1], line + at, side, result[at * side : (at + 1) * side])
    early, late = (out[0], out[1])
    first = product(early, early, ROWS)
    cross = product(early, late, ROWS)
    second = product(late, late, ROWS)
    packed = packed_corner(first, second)
    for at, block in enumerate((first[:PACK], cross[:PACK], cross[PACK:], second[:PACK], packed)):
        gram[at * PACK : (at + 1) * PACK, :] = block


def called(kernel, name, shapes, spaces, scratch, *args):
    spaces = list(spaces) + [pltpu.VMEM] * (len(args) - len(spaces))
    return pl.pallas_call(
        kernel,
        out_shape=[jax.ShapeDtypeStruct(shape, jnp.float32) for shape in shapes],
        in_specs=[pl.BlockSpec(memory_space=space) for space in spaces],
        out_specs=[pl.BlockSpec(memory_space=pltpu.VMEM)] * len(shapes),
        scratch_shapes=scratch,
        compiler_params=pltpu.CompilerParams(vmem_limit_bytes=24 * 1024 * 1024),
        name=name,
    )(*args)


def around(value):
    peers = lax.axis_size(LON)
    near = lax.ppermute(value, "core", [(0, 1), (1, 0)])
    across = [(i, (i + 1) % peers) for i in range(1, peers, 2)]
    return near, lax.ppermute(value, LON, across + [(j, i) for i, j in across])


def partnered(value):
    return lax.ppermute(value, "yh", [(0, 1), (1, 0)])


def passed_on(value):
    spots, halves = (lax.axis_size("x"), lax.axis_size("yh"))
    near = partnered(value)
    up = [(x * halves, (x + 1) * halves) for x in range(spots - 1)]
    down = [((x + 1) * halves + 1, x * halves + 1) for x in range(spots - 1)]
    return near, lax.ppermute(near, LAT, up + down)


def straight(value):
    across = [(at, at + 1) for at in range(1, lax.axis_size(LAT) - 1, 2)]
    return partnered(value), lax.ppermute(value, LAT, across + [(j, i) for i, j in across])


def body(field, lat_kernel, lon_kernel, time_taps):
    rows_lat, rows_lon, length_in = field.shape
    steps_out = length_in - 2 * TH
    lat_place = lax.axis_index(LAT)
    total_lat = rows_lat * lax.axis_size(LAT)
    local = rows_lat * rows_lon
    cells = local * lax.axis_size(LAT) * lax.axis_size(LON)
    tall = -(-rows_lon // STEP) * STEP
    globrow = (lat_place * rows_lat + jnp.arange(rows_lat, dtype=jnp.int32)).astype(jnp.float32)
    latitude = jnp.pi * (globrow + 0.5) / total_lat - jnp.pi / 2
    weights = jnp.sqrt(jnp.cos(latitude))
    half = (local, TILE)
    low = jnp.stack([lax.axis_index("yh") == 0, lax.axis_index("core") == 0]).astype(jnp.int32)
    padded = [pltpu.VMEM((rows_lat, tall, 2 * TILE), jnp.float32)]
    first, lat_row, lon_row = called(
        early_kernel,
        "early",
        [half, (1, 2 * SH + 1), (1, 2 * SH + 1)],
        [],
        padded,
        time_taps[None],
        lat_kernel[None],
        lon_kernel[None],
        field,
    )
    second, lat_band, lon_band, lat_weighted = called(
        late_kernel,
        "late",
        [half] + [(2 * SH, 6 * SH)] * 3,
        [pltpu.SMEM] * 2,
        padded,
        low,
        weights,
        time_taps[None],
        lat_row,
        lon_row,
        field,
    )
    smooth = functools.partial(smooth_kernel, SH)
    near, far = passed_on(first)
    beside, beyond = around(second)
    (second,) = called(smooth, "lon", [half], [], [], lon_band, beside, second, beyond)
    (first,) = called(smooth, "lat", [half], [], [], lat_band, near, first, far)
    near, far = straight(second)
    beside, beyond = around(first)
    matrix, local_gram = called(
        functools.partial(last_kernel, SH),
        "last",
        [(2,) + half, (5 * PACK, TILE)],
        [pltpu.SMEM],
        [],
        weights,
        lon_band,
        lat_weighted,
        beside,
        first,
        beyond,
        near,
        second,
        far,
    )
    gram = summed(local_gram)
    basis, merged = called(
        functools.partial(factor_kernel, cells),
        "factor",
        [(rows_lat, rows_lon, steps_out), (steps_out, steps_out)],
        [],
        [pltpu.VMEM((TILE, 2 * TILE), jnp.float32)],
        gram,
        matrix,
    )
    return (basis, merged)


def solution(mesh):
    fine = jax.sharding.Mesh(mesh.devices.reshape(4, 2, 2, 8, 2), ("x", "yh", "yl", "z", "core"))
    placed = (P(LAT, LON, None), P(), P(), P())
    return jax.shard_map(
        body, mesh=fine, in_specs=placed, out_specs=(P(LAT, LON, None), P()), check_vma=False
    )
```

```python
import functools

import jax
import jax.numpy as jnp
from jax import lax
from jax.experimental import pallas as pl
from jax.experimental.pallas import tpu as pltpu
from jax.sharding import PartitionSpec as P

TH = 64
SH = 20
LAT = ("x", "yh")
LON = ("yl", "z", "core")


PLANE = ("x", "yh", "yl", "core")


def shared(value, axes):
    peers = lax.axis_size(axes)
    copies = jnp.broadcast_to(value[None], (peers,) + value.shape)
    return lax.all_to_all(copies, axes, 0, 0)


def summed(value):
    peers = lax.axis_size(PLANE)
    pieces = lax.all_to_all(value.reshape(peers, 1, value.size // peers), PLANE, 0, 0)
    piece = shared(pieces.sum(axis=0), ("z",)).sum(axis=0)
    return shared(piece, PLANE).reshape(value.shape)


TILE = 128
STEP = 8
PACK = TILE // 2

def product(left, right, over):
    return lax.dot_general(
        left,
        right,
        (over, ((), ())),
        precision=lax.Precision.HIGHEST,
        preferred_element_type=jnp.float32,
    )


def wide(value):
    return jnp.broadcast_to(value, (STEP, TILE))


def eliminate(work):
    for top in range(0, TILE, STEP):
        flat = [wide(work[top + i:top + i + 1, :TILE]) for i in range(STEP)]
        left = {(i, j): wide(flat[i][:, top + j:top + j + 1]) for j in range(STEP) for i in range(j + 1)}
        rows = [[wide(work[top + i:top + i + 1, s:s + TILE]) for s in (0, TILE)] for i in range(STEP)]
        root, upper = [], {}
        for j in range(STEP):
            root.append(lax.rsqrt(left[j, j]))
            for i in range(j + 1, STEP):
                upper[j, i] = left[j, i] * root[j]
            for i in range(j + 1, STEP):
                for n in range(i, STEP):
                    left[i, n] = left[i, n] - upper[j, i] * upper[j, n]
        for j in range(STEP):
            rows[j] = [value * root[j] for value in rows[j]]
            for i in range(j + 1, STEP):
                rows[i] = [value - upper[j, i] * done for value, done in zip(rows[i], rows[j])]
        for j in range(STEP):
            for half in range(2):
                work[top + j:top + j + 1, half * TILE:(half + 1) * TILE] = rows[j][half][:1, :]
        for below in range(top + STEP, TILE, STEP):
            parts = [work[below:below + STEP, s:s + TILE] for s in (0, TILE)]
            factors = [wide(parts[0][:, top + j:top + j + 1]) for j in range(STEP)]
            for j in range(STEP):
                factors[j] = factors[j] * root[j]
                for i in range(j + 1, STEP):
                    factors[i] = factors[i] - upper[j, i] * factors[j]
            for half in range(2):
                terms = [factors[j] * rows[j][half] for j in range(STEP)]
                while len(terms) > 1:
                    terms = [one + other for one, other in zip(terms[::2], terms[1::2])]
                parts[half] = parts[half] - terms[0]
            for half in range(2):
                work[below:below + STEP, half * TILE:(half + 1) * TILE] = parts[half]


ROWS = ((0,), (0,))
COLS = ((1,), (1,))
PLAIN = ((1,), (0,))


def factor_kernel(cells, gram, early, late, basis, merged, work):
    row = lax.broadcasted_iota(jnp.int32, (TILE, TILE), 0)
    col = lax.broadcasted_iota(jnp.int32, (TILE, TILE), 1)
    eye = jnp.where(row == col, 1.0, 0.0).astype(jnp.float32)
    scale = float(cells) ** 0.5

    def solve(block):
        work[:, :TILE] = block
        work[:, TILE:] = eye
        eliminate(work)
        upper = jnp.where(row <= col, work[:, :TILE], 0.0)
        lower = jnp.where(row >= col, work[:, TILE:], 0.0)
        return upper, lower

    blocks = [gram[at * PACK : (at + 1) * PACK, :] for at in range(5)]
    r11, w11 = solve(mirrored(blocks[0], blocks[4]))
    r12 = product(w11, jnp.concatenate(blocks[1:3], axis=0), PLAIN)
    a22 = mirrored(blocks[3], pltpu.roll(blocks[4], PACK, 1)) - product(r12, r12, ROWS)
    left = product(early[...], w11, COLS)
    rest = late[...] - product(left, r12, PLAIN)
    r22, w22 = solve(a22)
    right = product(rest, w22 * scale, COLS)
    merged[:TILE, :TILE] = r11 * (1.0 / scale)
    merged[:TILE, TILE:] = r12 * (1.0 / scale)
    merged[TILE:, :TILE] = jnp.zeros((TILE, TILE), jnp.float32)
    merged[TILE:, TILE:] = r22 * (1.0 / scale)
    lines, side, _ = basis.shape
    for line in range(lines):
        part = slice(line * side, (line + 1) * side)
        basis[line, :, :TILE] = left[part] * scale
        basis[line, :, TILE:] = right[part]


def shifted(kernel, rows, start):
    flat = jnp.concatenate([kernel, jnp.zeros((1, TILE - kernel.shape[1]), jnp.float32)], axis=1)
    return pltpu.roll(jnp.broadcast_to(flat, (rows, TILE)), start, 1, stride=1, stride_axis=0)


def smoother(kernel, side):
    pair = 2 * side
    row = lax.broadcasted_iota(jnp.int32, (pair, TILE), 0)
    lane = lax.broadcasted_iota(jnp.int32, (pair, TILE), 1)
    total = jnp.zeros((pair, TILE), jnp.float32)
    for part in range(3):
        place = lane - part * pair
        inside = (place >= 0) & (place < pair) & ((place >= side) == (row >= side))
        total = jnp.where(inside, shifted(kernel, pair, part * side), total)
    return total[:, : 3 * pair]


def stacked(before, own, after, first, count):
    part = slice(first, first + count)
    return jnp.concatenate([lines[part, :] for lines in (before, own, after)], axis=0)


def turned(out, line, side, value):
    out[pl.ds(line, side, stride=out.shape[0] // side), :] = value


def ordered(first, kernel, side):
    pair = 2 * side
    plain = smoother(kernel[...], side)
    lead, middle, trail = (plain[:, at : at + pair] for at in (0, pair, 2 * pair))
    swapped = jnp.concatenate([trail, middle, lead], axis=1)
    return jnp.where(first == 1, swapped, plain)


def filtered(taps, field, padded, start):
    rows, cols, hours = padded.shape
    side = field.shape[1]
    count = taps.shape[1]
    lane = lax.broadcasted_iota(jnp.int32, (1, count), 1)
    full = taps[...] + jnp.where(lane == TH, 1.0, 0.0)
    full = jnp.concatenate([full, jnp.zeros((1, hours - count), jnp.float32)], axis=1)
    skew = pltpu.roll(jnp.broadcast_to(full, (TILE, hours)), 0, 1, stride=1, stride_axis=0)
    padded[:, side:, :] = jnp.zeros((rows, cols - side, hours), jnp.float32)
    padded[:, :side, :] = field[:, :, start : start + hours]
    return product(padded[...].reshape(rows * cols, hours), skew, COLS)


def early_kernel(taps, lat_kernel, lon_kernel, field, out, taps_out, lat_out, lon_out, padded):
    taps_out[...] = taps[...]
    lat_out[...] = lat_kernel[...]
    lon_out[...] = lon_kernel[...]
    rows, side, _ = field.shape
    result = filtered(taps, field, padded, 0)
    for row in range(rows):
        at = row * padded.shape[1]
        turned(out, row, side, result[at : at + side])


def late_kernel(taps, field, out, padded):
    rows, side, _ = field.shape
    result = filtered(taps, field, padded, TILE)
    for row in range(rows):
        at = row * padded.shape[1]
        out[row * side : (row + 1) * side, :] = result[at : at + side]


def bands_kernel(low, weights, lat_kernel, lon_kernel, lat_band, lon_band, lat_weighted):
    lat_band[...] = ordered(low[0], lat_kernel, SH)
    lon_band[...] = ordered(low[1], lon_kernel, SH)
    row = lax.broadcasted_iota(jnp.int32, (2 * SH, 1), 0)
    weight = jnp.zeros((2 * SH, 1), jnp.float32)
    for line in range(SH):
        weight = jnp.where((row == line) | (row == SH + line), weights[line], weight)
    lat_weighted[...] = lat_band[...] * weight


def smooth_kernel(side, band, near, own, far, out):
    pair = 2 * side
    for first in range(0, out.shape[0], pair):
        result = product(band[...], stacked(near, own, far, first, pair), PLAIN)
        for line in range(2):
            turned(out, first // side + line, side, result[line * side : (line + 1) * side])


def packed_corner(first, second):
    lane = lax.broadcasted_iota(jnp.int32, (PACK, TILE), 1)
    return jnp.where(lane < PACK, pltpu.roll(second[PACK:], PACK, 1), first[PACK:])


def mirrored(top, corner):
    row = lax.broadcasted_iota(jnp.int32, (TILE, TILE), 0)
    lane = lax.broadcasted_iota(jnp.int32, (TILE, TILE), 1)
    upper = jnp.concatenate([top, corner], axis=0)
    return jnp.where((row >= PACK) & (lane < PACK), upper.T, upper)


def early_last_kernel(side, weights, band, near, own, far, out, gram):
    pair = 2 * side
    row = lax.broadcasted_iota(jnp.int32, (pair, 1), 0)
    for first in range(0, out.shape[0], pair):
        line = first // side
        weight = jnp.where(row < side, weights[line], weights[line + 1])
        result = product(band[...], stacked(near, own, far, first, pair), PLAIN)
        out[first : first + pair, :] = result * weight
    gram[...] = product(out[...], out[...], ROWS)


def late_last_kernel(side, band, near, own, far, out, gram):
    smooth_kernel(side, band, near, own, far, out)
    gram[...] = product(out[...], out[...], ROWS)


def cross_kernel(early, late, early_gram, late_gram, gram):
    first, second = (early_gram[...], late_gram[...])
    cross = product(early[...], late[...], ROWS)
    packed = packed_corner(first, second)
    for at, block in enumerate((first[:PACK], cross[:PACK], cross[PACK:], second[:PACK], packed)):
        gram[at * PACK : (at + 1) * PACK, :] = block


def called(kernel, name, shapes, spaces, scratch, *args):
    spaces = list(spaces) + [pltpu.VMEM] * (len(args) - len(spaces))
    return pl.pallas_call(
        kernel,
        out_shape=[jax.ShapeDtypeStruct(shape, jnp.float32) for shape in shapes],
        in_specs=[pl.BlockSpec(memory_space=space) for space in spaces],
        out_specs=[pl.BlockSpec(memory_space=pltpu.VMEM)] * len(shapes),
        scratch_shapes=scratch,
        compiler_params=pltpu.CompilerParams(vmem_limit_bytes=24 * 1024 * 1024),
        name=name,
    )(*args)


def around(value):
    peers = lax.axis_size(LON)
    near = lax.ppermute(value, "core", [(0, 1), (1, 0)])
    across = [(i, (i + 1) % peers) for i in range(1, peers, 2)]
    return near, lax.ppermute(value, LON, across + [(j, i) for i, j in across])


def partnered(value):
    return lax.ppermute(value, "yh", [(0, 1), (1, 0)])


def handed_on(near):
    spots, halves = (lax.axis_size("x"), lax.axis_size("yh"))
    up = [(x * halves, (x + 1) * halves) for x in range(spots - 1)]
    down = [((x + 1) * halves + 1, x * halves + 1) for x in range(spots - 1)]
    return lax.ppermute(near, LAT, up + down)


def passed_on(value):
    near = partnered(value)
    return near, handed_on(near)


def straight(value):
    across = [(at, at + 1) for at in range(1, lax.axis_size(LAT) - 1, 2)]
    return partnered(value), lax.ppermute(value, LAT, across + [(j, i) for i, j in across])


def body(field, lat_kernel, lon_kernel, time_taps):
    rows_lat, rows_lon, length_in = field.shape
    steps_out = length_in - 2 * TH
    lat_place = lax.axis_index(LAT)
    total_lat = rows_lat * lax.axis_size(LAT)
    local = rows_lat * rows_lon
    cells = local * lax.axis_size(LAT) * lax.axis_size(LON)
    tall = -(-rows_lon // STEP) * STEP
    globrow = (lat_place * rows_lat + jnp.arange(rows_lat, dtype=jnp.int32)).astype(jnp.float32)
    latitude = jnp.pi * (globrow + 0.5) / total_lat - jnp.pi / 2
    weights = jnp.sqrt(jnp.cos(latitude))
    half = (local, TILE)
    low = jnp.stack([lax.axis_index("yh") == 0, lax.axis_index("core") == 0]).astype(jnp.int32)
    padded = [pltpu.VMEM((rows_lat, tall, 2 * TILE), jnp.float32)]
    first, taps_row, lat_row, lon_row = called(
        early_kernel,
        "early",
        [half, (1, 2 * TH + 1), (1, 2 * SH + 1), (1, 2 * SH + 1)],
        [],
        padded,
        time_taps[None],
        lat_kernel[None],
        lon_kernel[None],
        field,
    )
    (second,) = called(late_kernel, "late", [half], [], padded, taps_row, field)
    lat_band, lon_band, lat_weighted = called(
        bands_kernel, "bands", [(2 * SH, 6 * SH)] * 3, [pltpu.SMEM] * 2, [], low, weights, lat_row, lon_row
    )
    smooth = functools.partial(smooth_kernel, SH)
    near, far = passed_on(first)
    beside, beyond = around(second)
    (second,) = called(smooth, "lon", [half], [], [], lon_band, beside, second, beyond)
    close, distant = straight(second)
    (first,) = called(smooth, "lat", [half], [], [], lat_band, near, first, far)
    beside, beyond = around(first)
    early, early_gram = called(
        functools.partial(early_last_kernel, SH),
        "first",
        [half, (TILE, TILE)],
        [pltpu.SMEM],
        [],
        weights,
        lon_band,
        beside,
        first,
        beyond,
    )
    late, late_gram = called(
        functools.partial(late_last_kernel, SH),
        "second",
        [half, (TILE, TILE)],
        [],
        [],
        lat_weighted,
        close,
        second,
        distant,
    )
    (local_gram,) = called(
        cross_kernel, "cross", [(5 * PACK, TILE)], [], [], early, late, early_gram, late_gram
    )
    gram = summed(local_gram)
    basis, merged = called(
        functools.partial(factor_kernel, cells),
        "factor",
        [(rows_lat, rows_lon, steps_out), (steps_out, steps_out)],
        [],
        [pltpu.VMEM((TILE, 2 * TILE), jnp.float32)],
        gram,
        early,
        late,
    )
    return (basis, merged)


def solution(mesh):
    fine = jax.sharding.Mesh(mesh.devices.reshape(4, 2, 2, 8, 2), ("x", "yh", "yl", "z", "core"))
    placed = (P(LAT, LON, None), P(), P(), P())
    return jax.shard_map(
        body, mesh=fine, in_specs=placed, out_specs=(P(LAT, LON, None), P()), check_vma=False
    )
```

```python
import functools

import jax
import jax.numpy as jnp
from jax import lax
from jax.experimental import pallas as pl
from jax.experimental.pallas import tpu as pltpu
from jax.sharding import PartitionSpec as P

TH = 64
SH = 20
LAT = ("x", "yh")
LON = ("yl", "z", "core")


PLANE = ("x", "yh", "yl", "core")


def shared(value, axes):
    peers = lax.axis_size(axes)
    copies = jnp.broadcast_to(value[None], (peers,) + value.shape)
    return lax.all_to_all(copies, axes, 0, 0)


def summed(value):
    peers = lax.axis_size(PLANE)
    pieces = lax.all_to_all(value.reshape(peers, 1, value.size // peers), PLANE, 0, 0)
    piece = shared(pieces.sum(axis=0), ("z",)).sum(axis=0)
    return shared(piece, PLANE).reshape(value.shape)


TILE = 128
STEP = 8
PACK = TILE // 2

def product(left, right, over):
    return lax.dot_general(
        left,
        right,
        (over, ((), ())),
        precision=lax.Precision.HIGHEST,
        preferred_element_type=jnp.float32,
    )


def wide(value):
    return jnp.broadcast_to(value, (STEP, TILE))


def eliminate(work):
    for top in range(0, TILE, STEP):
        flat = [wide(work[top + i:top + i + 1, :TILE]) for i in range(STEP)]
        left = {(i, j): wide(flat[i][:, top + j:top + j + 1]) for j in range(STEP) for i in range(j + 1)}
        rows = [[wide(work[top + i:top + i + 1, s:s + TILE]) for s in (0, TILE)] for i in range(STEP)]
        root, upper = [], {}
        for j in range(STEP):
            root.append(lax.rsqrt(left[j, j]))
            for i in range(j + 1, STEP):
                upper[j, i] = left[j, i] * root[j]
            for i in range(j + 1, STEP):
                for n in range(i, STEP):
                    left[i, n] = left[i, n] - upper[j, i] * upper[j, n]
        for j in range(STEP):
            rows[j] = [value * root[j] for value in rows[j]]
            for i in range(j + 1, STEP):
                rows[i] = [value - upper[j, i] * done for value, done in zip(rows[i], rows[j])]
        for j in range(STEP):
            for half in range(2):
                work[top + j:top + j + 1, half * TILE:(half + 1) * TILE] = rows[j][half][:1, :]
        for below in range(top + STEP, TILE, STEP):
            parts = [work[below:below + STEP, s:s + TILE] for s in (0, TILE)]
            factors = [wide(parts[0][:, top + j:top + j + 1]) for j in range(STEP)]
            for j in range(STEP):
                factors[j] = factors[j] * root[j]
                for i in range(j + 1, STEP):
                    factors[i] = factors[i] - upper[j, i] * factors[j]
            for half in range(2):
                terms = [factors[j] * rows[j][half] for j in range(STEP)]
                while len(terms) > 1:
                    terms = [one + other for one, other in zip(terms[::2], terms[1::2])]
                parts[half] = parts[half] - terms[0]
            for half in range(2):
                work[below:below + STEP, half * TILE:(half + 1) * TILE] = parts[half]


ROWS = ((0,), (0,))
COLS = ((1,), (1,))
PLAIN = ((1,), (0,))


def factor_kernel(cells, gram, matrix, basis, merged, work):
    row = lax.broadcasted_iota(jnp.int32, (TILE, TILE), 0)
    col = lax.broadcasted_iota(jnp.int32, (TILE, TILE), 1)
    eye = jnp.where(row == col, 1.0, 0.0).astype(jnp.float32)
    scale = float(cells) ** 0.5

    def solve(block):
        work[:, :TILE] = block
        work[:, TILE:] = eye
        eliminate(work)
        upper = jnp.where(row <= col, work[:, :TILE], 0.0)
        lower = jnp.where(row >= col, work[:, TILE:], 0.0)
        return upper, lower

    blocks = [gram[at * PACK : (at + 1) * PACK, :] for at in range(5)]
    r11, w11 = solve(mirrored(blocks[0], blocks[4]))
    r12 = product(w11, jnp.concatenate(blocks[1:3], axis=0), PLAIN)
    a22 = mirrored(blocks[3], pltpu.roll(blocks[4], PACK, 1)) - product(r12, r12, ROWS)
    left = product(matrix[0], w11, COLS)
    rest = matrix[1] - product(left, r12, PLAIN)
    r22, w22 = solve(a22)
    right = product(rest, w22 * scale, COLS)
    merged[:TILE, :TILE] = r11 * (1.0 / scale)
    merged[:TILE, TILE:] = r12 * (1.0 / scale)
    merged[TILE:, :TILE] = jnp.zeros((TILE, TILE), jnp.float32)
    merged[TILE:, TILE:] = r22 * (1.0 / scale)
    lines, side, _ = basis.shape
    for line in range(lines):
        part = slice(line * side, (line + 1) * side)
        basis[line, :, :TILE] = left[part] * scale
        basis[line, :, TILE:] = right[part]


def shifted(kernel, rows, start):
    flat = jnp.concatenate([kernel, jnp.zeros((1, TILE - kernel.shape[1]), jnp.float32)], axis=1)
    return pltpu.roll(jnp.broadcast_to(flat, (rows, TILE)), start, 1, stride=1, stride_axis=0)


def smoother(kernel, side):
    pair = 2 * side
    row = lax.broadcasted_iota(jnp.int32, (pair, TILE), 0)
    lane = lax.broadcasted_iota(jnp.int32, (pair, TILE), 1)
    total = jnp.zeros((pair, TILE), jnp.float32)
    for part in range(3):
        place = lane - part * pair
        inside = (place >= 0) & (place < pair) & ((place >= side) == (row >= side))
        total = jnp.where(inside, shifted(kernel, pair, part * side), total)
    return total[:, : 3 * pair]


def stacked(before, own, after, first, count):
    part = slice(first, first + count)
    return jnp.concatenate([lines[part, :] for lines in (before, own, after)], axis=0)


def turned(out, line, side, value):
    out[pl.ds(line, side, stride=out.shape[0] // side), :] = value


def ordered(first, kernel, side):
    pair = 2 * side
    plain = smoother(kernel[...], side)
    lead, middle, trail = (plain[:, at : at + pair] for at in (0, pair, 2 * pair))
    swapped = jnp.concatenate([trail, middle, lead], axis=1)
    return jnp.where(first == 1, swapped, plain)


def filtered(taps, field, padded, start):
    rows, cols, hours = padded.shape
    side = field.shape[1]
    count = taps.shape[1]
    lane = lax.broadcasted_iota(jnp.int32, (1, count), 1)
    full = taps[...] + jnp.where(lane == TH, 1.0, 0.0)
    full = jnp.concatenate([full, jnp.zeros((1, hours - count), jnp.float32)], axis=1)
    skew = pltpu.roll(jnp.broadcast_to(full, (TILE, hours)), 0, 1, stride=1, stride_axis=0)
    padded[:, side:, :] = jnp.zeros((rows, cols - side, hours), jnp.float32)
    padded[:, :side, :] = field[:, :, start : start + hours]
    return product(padded[...].reshape(rows * cols, hours), skew, COLS)


def early_kernel(taps, lat_kernel, lon_kernel, field, out, lat_out, lon_out, padded):
    lat_out[...] = lat_kernel[...]
    lon_out[...] = lon_kernel[...]
    rows, side, _ = field.shape
    result = filtered(taps, field, padded, 0)
    for row in range(rows):
        at = row * padded.shape[1]
        turned(out, row, side, result[at : at + side])


def late_kernel(low, weights, taps, lat_kernel, lon_kernel, field, out, lat_band, lon_band, padded):
    rows, side, _ = field.shape
    result = filtered(taps, field, padded, TILE)
    for row in range(rows):
        at = row * padded.shape[1]
        out[row * side : (row + 1) * side, :] = result[at : at + side]
    lon_band[...] = ordered(low[1], lon_kernel, SH)
    row = lax.broadcasted_iota(jnp.int32, (2 * SH, 1), 0)
    weight = jnp.zeros((2 * SH, 1), jnp.float32)
    for line in range(SH):
        weight = jnp.where((row == line) | (row == SH + line), weights[line], weight)
    lat_band[...] = ordered(low[0], lat_kernel, SH) * weight


def smooth_kernel(side, band, near, own, far, out):
    pair = 2 * side
    for first in range(0, out.shape[0], pair):
        result = product(band[...], stacked(near, own, far, first, pair), PLAIN)
        for line in range(2):
            turned(out, first // side + line, side, result[line * side : (line + 1) * side])


def packed_corner(first, second):
    lane = lax.broadcasted_iota(jnp.int32, (PACK, TILE), 1)
    return jnp.where(lane < PACK, pltpu.roll(second[PACK:], PACK, 1), first[PACK:])


def mirrored(top, corner):
    row = lax.broadcasted_iota(jnp.int32, (TILE, TILE), 0)
    lane = lax.broadcasted_iota(jnp.int32, (TILE, TILE), 1)
    upper = jnp.concatenate([top, corner], axis=0)
    return jnp.where((row >= PACK) & (lane < PACK), upper.T, upper)


def last_kernel(side, lon_band, lat_band, *refs):
    parts, (out, gram) = (refs[:-2], refs[-2:])
    pair = 2 * side
    for first in range(0, out.shape[1], pair):
        line = first // side
        out[0, first : first + pair, :] = product(lon_band[...], stacked(*parts[:3], first, pair), PLAIN)
        result = product(lat_band[...], stacked(*parts[3:], first, pair), PLAIN)
        for at in range(2):
            turned(out.at[1], line + at, side, result[at * side : (at + 1) * side])
    early, late = (out[0], out[1])
    first = product(early, early, ROWS)
    cross = product(early, late, ROWS)
    second = product(late, late, ROWS)
    packed = packed_corner(first, second)
    for at, block in enumerate((first[:PACK], cross[:PACK], cross[PACK:], second[:PACK], packed)):
        gram[at * PACK : (at + 1) * PACK, :] = block


def called(kernel, name, shapes, spaces, scratch, *args):
    spaces = list(spaces) + [pltpu.VMEM] * (len(args) - len(spaces))
    return pl.pallas_call(
        kernel,
        out_shape=[jax.ShapeDtypeStruct(shape, jnp.float32) for shape in shapes],
        in_specs=[pl.BlockSpec(memory_space=space) for space in spaces],
        out_specs=[pl.BlockSpec(memory_space=pltpu.VMEM)] * len(shapes),
        scratch_shapes=scratch,
        compiler_params=pltpu.CompilerParams(vmem_limit_bytes=24 * 1024 * 1024),
        name=name,
    )(*args)


def around(value):
    peers = lax.axis_size(LON)
    near = lax.ppermute(value, "core", [(0, 1), (1, 0)])
    across = [(i, (i + 1) % peers) for i in range(1, peers, 2)]
    return near, lax.ppermute(value, LON, across + [(j, i) for i, j in across])


def partnered(value):
    return lax.ppermute(value, "yh", [(0, 1), (1, 0)])


def passed_on(value):
    spots, halves = (lax.axis_size("x"), lax.axis_size("yh"))
    near = partnered(value)
    up = [(x * halves, (x + 1) * halves) for x in range(spots - 1)]
    down = [((x + 1) * halves + 1, x * halves + 1) for x in range(spots - 1)]
    return near, lax.ppermute(near, LAT, up + down)


def straight(value):
    across = [(at, at + 1) for at in range(1, lax.axis_size(LAT) - 1, 2)]
    return partnered(value), lax.ppermute(value, LAT, across + [(j, i) for i, j in across])


def body(field, lat_kernel, lon_kernel, time_taps):
    rows_lat, rows_lon, length_in = field.shape
    steps_out = length_in - 2 * TH
    lat_place = lax.axis_index(LAT)
    total_lat = rows_lat * lax.axis_size(LAT)
    local = rows_lat * rows_lon
    cells = local * lax.axis_size(LAT) * lax.axis_size(LON)
    tall = -(-rows_lon // STEP) * STEP
    globrow = (lat_place * rows_lat + jnp.arange(rows_lat, dtype=jnp.int32)).astype(jnp.float32)
    latitude = jnp.pi * (globrow + 0.5) / total_lat - jnp.pi / 2
    weights = jnp.sqrt(jnp.cos(latitude))
    half = (local, TILE)
    low = jnp.stack([lax.axis_index("yh") == 0, lax.axis_index("core") == 0]).astype(jnp.int32)
    padded = [pltpu.VMEM((rows_lat, tall, 2 * TILE), jnp.float32)]
    first, lat_row, lon_row = called(
        early_kernel,
        "early",
        [half, (1, 2 * SH + 1), (1, 2 * SH + 1)],
        [],
        padded,
        time_taps[None],
        lat_kernel[None],
        lon_kernel[None],
        field,
    )
    second, lat_band, lon_band = called(
        late_kernel,
        "late",
        [half] + [(2 * SH, 6 * SH)] * 2,
        [pltpu.SMEM] * 2,
        padded,
        low,
        weights,
        time_taps[None],
        lat_row,
        lon_row,
        field,
    )
    smooth = functools.partial(smooth_kernel, SH)
    near, far = passed_on(first)
    beside, beyond = around(second)
    (second,) = called(smooth, "lon", [half], [], [], lon_band, beside, second, beyond)
    (first,) = called(smooth, "lat", [half], [], [], lat_band, near, first, far)
    near, far = straight(second)
    beside, beyond = around(first)
    matrix, local_gram = called(
        functools.partial(last_kernel, SH),
        "last",
        [(2,) + half, (5 * PACK, TILE)],
        [],
        [],
        lon_band,
        lat_band,
        beside,
        first,
        beyond,
        near,
        second,
        far,
    )
    gram = summed(local_gram)
    basis, merged = called(
        functools.partial(factor_kernel, cells),
        "factor",
        [(rows_lat, rows_lon, steps_out), (steps_out, steps_out)],
        [],
        [pltpu.VMEM((TILE, 2 * TILE), jnp.float32)],
        gram,
        matrix,
    )
    return (basis, merged)


def solution(mesh):
    fine = jax.sharding.Mesh(mesh.devices.reshape(4, 2, 2, 8, 2), ("x", "yh", "yl", "z", "core"))
    placed = (P(LAT, LON, None), P(), P(), P())
    return jax.shard_map(
        body, mesh=fine, in_specs=placed, out_specs=(P(LAT, LON, None), P()), check_vma=False
    )
```

```python
import functools

import jax
import jax.numpy as jnp
from jax import lax
from jax.experimental import pallas as pl
from jax.experimental.pallas import tpu as pltpu
from jax.sharding import PartitionSpec as P

TH = 64
SH = 20
LAT = ("x", "yh")
LON = ("yl", "z", "core")


PLANE = ("x", "yh", "yl", "core")


def shared(value, axes):
    peers = lax.axis_size(axes)
    copies = jnp.broadcast_to(value[None], (peers,) + value.shape)
    return lax.all_to_all(copies, axes, 0, 0)


def summed(value):
    peers = lax.axis_size(PLANE)
    pieces = lax.all_to_all(value.reshape(peers, 1, value.size // peers), PLANE, 0, 0)
    piece = shared(pieces.sum(axis=0), ("z",)).sum(axis=0)
    return shared(piece, PLANE).reshape(value.shape)


TILE = 128
STEP = 8
PACK = TILE // 2

def product(left, right, over):
    return lax.dot_general(
        left,
        right,
        (over, ((), ())),
        precision=lax.Precision.HIGHEST,
        preferred_element_type=jnp.float32,
    )


def wide(value):
    return jnp.broadcast_to(value, (STEP, TILE))


def eliminate(work, tasks=()):
    for top in range(0, TILE, STEP):
        for task in tasks[top // STEP : top // STEP + 1]:
            task()
        flat = [wide(work[top + i:top + i + 1, :TILE]) for i in range(STEP)]
        left = {(i, j): wide(flat[i][:, top + j:top + j + 1]) for j in range(STEP) for i in range(j + 1)}
        rows = [[wide(work[top + i:top + i + 1, s:s + TILE]) for s in (0, TILE)] for i in range(STEP)]
        root, upper = [], {}
        for j in range(STEP):
            root.append(lax.rsqrt(left[j, j]))
            for i in range(j + 1, STEP):
                upper[j, i] = left[j, i] * root[j]
            for i in range(j + 1, STEP):
                for n in range(i, STEP):
                    left[i, n] = left[i, n] - upper[j, i] * upper[j, n]
        for j in range(STEP):
            rows[j] = [value * root[j] for value in rows[j]]
            for i in range(j + 1, STEP):
                rows[i] = [value - upper[j, i] * done for value, done in zip(rows[i], rows[j])]
        for j in range(STEP):
            for half in range(2):
                work[top + j:top + j + 1, half * TILE:(half + 1) * TILE] = rows[j][half][:1, :]
        for below in range(top + STEP, TILE, STEP):
            parts = [work[below:below + STEP, s:s + TILE] for s in (0, TILE)]
            factors = [wide(parts[0][:, top + j:top + j + 1]) for j in range(STEP)]
            for j in range(STEP):
                factors[j] = factors[j] * root[j]
                for i in range(j + 1, STEP):
                    factors[i] = factors[i] - upper[j, i] * factors[j]
            for half in range(2):
                terms = [factors[j] * rows[j][half] for j in range(STEP)]
                while len(terms) > 1:
                    terms = [one + other for one, other in zip(terms[::2], terms[1::2])]
                parts[half] = parts[half] - terms[0]
            for half in range(2):
                work[below:below + STEP, half * TILE:(half + 1) * TILE] = parts[half]


ROWS = ((0,), (0,))
COLS = ((1,), (1,))
PLAIN = ((1,), (0,))


def factor_kernel(cells, gram, matrix, basis, merged, work):
    row = lax.broadcasted_iota(jnp.int32, (TILE, TILE), 0)
    col = lax.broadcasted_iota(jnp.int32, (TILE, TILE), 1)
    eye = jnp.where(row == col, 1.0, 0.0).astype(jnp.float32)
    scale = float(cells) ** 0.5

    def solve(block, tasks=()):
        work[:, :TILE] = block
        work[:, TILE:] = eye
        eliminate(work, tasks)
        upper = jnp.where(row <= col, work[:, :TILE], 0.0)
        lower = jnp.where(row >= col, work[:, TILE:], 0.0)
        return upper, lower

    blocks = [gram[at * PACK : (at + 1) * PACK, :] for at in range(5)]
    r11, w11 = solve(mirrored(blocks[0], blocks[4]))
    r12 = product(w11, jnp.concatenate(blocks[1:3], axis=0), PLAIN)
    a22 = mirrored(blocks[3], pltpu.roll(blocks[4], PACK, 1)) - product(r12, r12, ROWS)
    first, second = (matrix[0], matrix[1])
    lines, side, _ = basis.shape
    count = 4
    rest = []

    def early_part(start):
        part = slice(start * side, (start + count) * side)
        left = product(first[part], w11, COLS)
        rest.append(second[part] - product(left, r12, PLAIN))
        for line in range(count):
            basis[start + line, :, :TILE] = left[line * side : (line + 1) * side] * scale

    tasks = [functools.partial(early_part, start) for start in range(0, lines, count)]
    r22, w22 = solve(a22, tasks)
    right = product(jnp.concatenate(rest, axis=0), w22 * scale, COLS)
    merged[:TILE, :TILE] = r11 * (1.0 / scale)
    merged[:TILE, TILE:] = r12 * (1.0 / scale)
    merged[TILE:, :TILE] = jnp.zeros((TILE, TILE), jnp.float32)
    merged[TILE:, TILE:] = r22 * (1.0 / scale)
    for line in range(lines):
        part = slice(line * side, (line + 1) * side)
        basis[line, :, TILE:] = right[part]


def shifted(kernel, rows, start):
    flat = jnp.concatenate([kernel, jnp.zeros((1, TILE - kernel.shape[1]), jnp.float32)], axis=1)
    return pltpu.roll(jnp.broadcast_to(flat, (rows, TILE)), start, 1, stride=1, stride_axis=0)


def smoother(kernel, side):
    pair = 2 * side
    row = lax.broadcasted_iota(jnp.int32, (pair, TILE), 0)
    lane = lax.broadcasted_iota(jnp.int32, (pair, TILE), 1)
    total = jnp.zeros((pair, TILE), jnp.float32)
    for part in range(3):
        place = lane - part * pair
        inside = (place >= 0) & (place < pair) & ((place >= side) == (row >= side))
        total = jnp.where(inside, shifted(kernel, pair, part * side), total)
    return total[:, : 3 * pair]


def stacked(before, own, after, first, count):
    part = slice(first, first + count)
    return jnp.concatenate([lines[part, :] for lines in (before, own, after)], axis=0)


def turned(out, line, side, value):
    out[pl.ds(line, side, stride=out.shape[0] // side), :] = value


def ordered(first, kernel, side):
    pair = 2 * side
    plain = smoother(kernel[...], side)
    lead, middle, trail = (plain[:, at : at + pair] for at in (0, pair, 2 * pair))
    swapped = jnp.concatenate([trail, middle, lead], axis=1)
    return jnp.where(first == 1, swapped, plain)


def filtered(taps, field, padded, start):
    rows, cols, hours = padded.shape
    side = field.shape[1]
    count = taps.shape[1]
    lane = lax.broadcasted_iota(jnp.int32, (1, count), 1)
    full = taps[...] + jnp.where(lane == TH, 1.0, 0.0)
    full = jnp.concatenate([full, jnp.zeros((1, hours - count), jnp.float32)], axis=1)
    skew = pltpu.roll(jnp.broadcast_to(full, (TILE, hours)), 0, 1, stride=1, stride_axis=0)
    padded[:, side:, :] = jnp.zeros((rows, cols - side, hours), jnp.float32)
    padded[:, :side, :] = field[:, :, start : start + hours]
    return product(padded[...].reshape(rows * cols, hours), skew, COLS)


def early_kernel(taps, lat_kernel, lon_kernel, field, out, lat_out, lon_out, padded):
    lat_out[...] = lat_kernel[...]
    lon_out[...] = lon_kernel[...]
    rows, side, _ = field.shape
    result = filtered(taps, field, padded, 0)
    for row in range(rows):
        at = row * padded.shape[1]
        turned(out, row, side, result[at : at + side])


def late_kernel(low, weights, taps, lat_kernel, lon_kernel, field, out, lat_band, lon_band, padded):
    rows, side, _ = field.shape
    result = filtered(taps, field, padded, TILE)
    for row in range(rows):
        at = row * padded.shape[1]
        out[row * side : (row + 1) * side, :] = result[at : at + side]
    lon_band[...] = ordered(low[1], lon_kernel, SH)
    lat_band[...] = ordered(low[0], lat_kernel, SH) * weights[...]


def smooth_kernel(side, band, near, own, far, out):
    pair = 2 * side
    for first in range(0, out.shape[0], pair):
        result = product(band[...], stacked(near, own, far, first, pair), PLAIN)
        for line in range(2):
            turned(out, first // side + line, side, result[line * side : (line + 1) * side])


def packed_corner(first, second):
    lane = lax.broadcasted_iota(jnp.int32, (PACK, TILE), 1)
    return jnp.where(lane < PACK, pltpu.roll(second[PACK:], PACK, 1), first[PACK:])


def mirrored(top, corner):
    row = lax.broadcasted_iota(jnp.int32, (TILE, TILE), 0)
    lane = lax.broadcasted_iota(jnp.int32, (TILE, TILE), 1)
    upper = jnp.concatenate([top, corner], axis=0)
    return jnp.where((row >= PACK) & (lane < PACK), upper.T, upper)


def last_kernel(side, lon_band, lat_band, *refs):
    parts, (out, gram) = (refs[:-2], refs[-2:])
    pair = 2 * side
    for first in range(0, out.shape[1], pair):
        line = first // side
        out[0, first : first + pair, :] = product(lon_band[...], stacked(*parts[:3], first, pair), PLAIN)
        result = product(lat_band[...], stacked(*parts[3:], first, pair), PLAIN)
        for at in range(2):
            turned(out.at[1], line + at, side, result[at * side : (at + 1) * side])
    early, late = (out[0], out[1])
    first = product(early, early, ROWS)
    cross = product(early, late, ROWS)
    second = product(late, late, ROWS)
    packed = packed_corner(first, second)
    for at, block in enumerate((first[:PACK], cross[:PACK], cross[PACK:], second[:PACK], packed)):
        gram[at * PACK : (at + 1) * PACK, :] = block


def called(kernel, name, shapes, spaces, scratch, *args):
    spaces = list(spaces) + [pltpu.VMEM] * (len(args) - len(spaces))
    return pl.pallas_call(
        kernel,
        out_shape=[jax.ShapeDtypeStruct(shape, jnp.float32) for shape in shapes],
        in_specs=[pl.BlockSpec(memory_space=space) for space in spaces],
        out_specs=[pl.BlockSpec(memory_space=pltpu.VMEM)] * len(shapes),
        scratch_shapes=scratch,
        compiler_params=pltpu.CompilerParams(vmem_limit_bytes=24 * 1024 * 1024),
        name=name,
    )(*args)


def around(value):
    peers = lax.axis_size(LON)
    near = lax.ppermute(value, "core", [(0, 1), (1, 0)])
    across = [(i, (i + 1) % peers) for i in range(1, peers, 2)]
    return near, lax.ppermute(value, LON, across + [(j, i) for i, j in across])


def partnered(value):
    return lax.ppermute(value, "yh", [(0, 1), (1, 0)])


def passed_on(value):
    spots, halves = (lax.axis_size("x"), lax.axis_size("yh"))
    near = partnered(value)
    up = [(x * halves, (x + 1) * halves) for x in range(spots - 1)]
    down = [((x + 1) * halves + 1, x * halves + 1) for x in range(spots - 1)]
    return near, lax.ppermute(near, LAT, up + down)


def straight(value):
    across = [(at, at + 1) for at in range(1, lax.axis_size(LAT) - 1, 2)]
    return partnered(value), lax.ppermute(value, LAT, across + [(j, i) for i, j in across])


def body(field, lat_kernel, lon_kernel, time_taps):
    rows_lat, rows_lon, length_in = field.shape
    steps_out = length_in - 2 * TH
    lat_place = lax.axis_index(LAT)
    total_lat = rows_lat * lax.axis_size(LAT)
    local = rows_lat * rows_lon
    cells = local * lax.axis_size(LAT) * lax.axis_size(LON)
    tall = -(-rows_lon // STEP) * STEP
    line = lax.broadcasted_iota(jnp.int32, (2 * rows_lat, 1), 0) % rows_lat
    globrow = (lat_place * rows_lat + line).astype(jnp.float32)
    latitude = jnp.pi * (globrow + 0.5) / total_lat - jnp.pi / 2
    weights = jnp.sqrt(jnp.cos(latitude))
    half = (local, TILE)
    low = jnp.stack([lax.axis_index("yh") == 0, lax.axis_index("core") == 0]).astype(jnp.int32)
    padded = [pltpu.VMEM((rows_lat, tall, 2 * TILE), jnp.float32)]
    first, lat_row, lon_row = called(
        early_kernel,
        "early",
        [half, (1, 2 * SH + 1), (1, 2 * SH + 1)],
        [],
        padded,
        time_taps[None],
        lat_kernel[None],
        lon_kernel[None],
        field,
    )
    second, lat_band, lon_band = called(
        late_kernel,
        "late",
        [half] + [(2 * SH, 6 * SH)] * 2,
        [pltpu.SMEM],
        padded,
        low,
        weights,
        time_taps[None],
        lat_row,
        lon_row,
        field,
    )
    smooth = functools.partial(smooth_kernel, SH)
    near, far = passed_on(first)
    beside, beyond = around(second)
    (second,) = called(smooth, "lon", [half], [], [], lon_band, beside, second, beyond)
    (first,) = called(smooth, "lat", [half], [], [], lat_band, near, first, far)
    near, far = straight(second)
    beside, beyond = around(first)
    matrix, local_gram = called(
        functools.partial(last_kernel, SH),
        "last",
        [(2,) + half, (5 * PACK, TILE)],
        [],
        [],
        lon_band,
        lat_band,
        beside,
        first,
        beyond,
        near,
        second,
        far,
    )
    gram = summed(local_gram)
    basis, merged = called(
        functools.partial(factor_kernel, cells),
        "factor",
        [(rows_lat, rows_lon, steps_out), (steps_out, steps_out)],
        [],
        [pltpu.VMEM((TILE, 2 * TILE), jnp.float32)],
        gram,
        matrix,
    )
    return (basis, merged)


def solution(mesh):
    fine = jax.sharding.Mesh(mesh.devices.reshape(4, 2, 2, 8, 2), ("x", "yh", "yl", "z", "core"))
    placed = (P(LAT, LON, None), P(), P(), P())
    return jax.shard_map(
        body, mesh=fine, in_specs=placed, out_specs=(P(LAT, LON, None), P()), check_vma=False
    )
```

```python
import functools

import jax
import jax.numpy as jnp
from jax import lax
from jax.experimental import pallas as pl
from jax.experimental.pallas import tpu as pltpu
from jax.sharding import PartitionSpec as P

TH = 64
SH = 20
LAT = ("x", "yh")
LON = ("yl", "z", "core")


PLANE = ("x", "yh", "yl", "core")


def shared(value, axes):
    peers = lax.axis_size(axes)
    copies = jnp.broadcast_to(value[None], (peers,) + value.shape)
    return lax.all_to_all(copies, axes, 0, 0)


def summed(value):
    peers = lax.axis_size(PLANE)
    pieces = lax.all_to_all(value.reshape(peers, 1, value.size // peers), PLANE, 0, 0)
    piece = shared(pieces.sum(axis=0), ("z",)).sum(axis=0)
    return shared(piece, PLANE).reshape(value.shape)


TILE = 128
STEP = 8
PACK = TILE // 2

def product(left, right, over):
    return lax.dot_general(
        left,
        right,
        (over, ((), ())),
        precision=lax.Precision.HIGHEST,
        preferred_element_type=jnp.float32,
    )


def wide(value):
    return jnp.broadcast_to(value, (STEP, TILE))


def eliminate(work, tasks=()):
    for top in range(0, TILE, STEP):
        for task in tasks[top // STEP : top // STEP + 1]:
            task()
        flat = [wide(work[top + i:top + i + 1, :TILE]) for i in range(STEP)]
        left = {(i, j): wide(flat[i][:, top + j:top + j + 1]) for j in range(STEP) for i in range(j + 1)}
        rows = [[wide(work[top + i:top + i + 1, s:s + TILE]) for s in (0, TILE)] for i in range(STEP)]
        root, upper = [], {}
        for j in range(STEP):
            root.append(lax.rsqrt(left[j, j]))
            for i in range(j + 1, STEP):
                upper[j, i] = left[j, i] * root[j]
            for i in range(j + 1, STEP):
                for n in range(i, STEP):
                    left[i, n] = left[i, n] - upper[j, i] * upper[j, n]
        for j in range(STEP):
            rows[j] = [value * root[j] for value in rows[j]]
            for i in range(j + 1, STEP):
                rows[i] = [value - upper[j, i] * done for value, done in zip(rows[i], rows[j])]
        for j in range(STEP):
            for half in range(2):
                work[top + j:top + j + 1, half * TILE:(half + 1) * TILE] = rows[j][half][:1, :]
        for below in range(top + STEP, TILE, STEP):
            parts = [work[below:below + STEP, s:s + TILE] for s in (0, TILE)]
            factors = [wide(parts[0][:, top + j:top + j + 1]) for j in range(STEP)]
            for j in range(STEP):
                factors[j] = factors[j] * root[j]
                for i in range(j + 1, STEP):
                    factors[i] = factors[i] - upper[j, i] * factors[j]
            for half in range(2):
                terms = [factors[j] * rows[j][half] for j in range(STEP)]
                while len(terms) > 1:
                    terms = [one + other for one, other in zip(terms[::2], terms[1::2])]
                parts[half] = parts[half] - terms[0]
            for half in range(2):
                work[below:below + STEP, half * TILE:(half + 1) * TILE] = parts[half]


ROWS = ((0,), (0,))
COLS = ((1,), (1,))
PLAIN = ((1,), (0,))


def factor_kernel(cells, gram, matrix, basis, merged, work):
    row = lax.broadcasted_iota(jnp.int32, (TILE, TILE), 0)
    col = lax.broadcasted_iota(jnp.int32, (TILE, TILE), 1)
    eye = jnp.where(row == col, 1.0, 0.0).astype(jnp.float32)
    scale = float(cells) ** 0.5

    def solve(block, tasks=()):
        work[:, :TILE] = block
        work[:, TILE:] = eye
        eliminate(work, tasks)
        upper = jnp.where(row <= col, work[:, :TILE], 0.0)
        lower = jnp.where(row >= col, work[:, TILE:], 0.0)
        return upper, lower

    blocks = [gram[at * PACK : (at + 1) * PACK, :] for at in range(5)]
    r11, w11 = solve(mirrored(blocks[0], blocks[4]))
    r12 = product(w11, jnp.concatenate(blocks[1:3], axis=0), PLAIN)
    a22 = mirrored(blocks[3], pltpu.roll(blocks[4], PACK, 1)) - product(r12, r12, ROWS)
    first, second = (matrix[0], matrix[1])
    lines, side, _ = basis.shape
    count = 4
    rest = []

    def early_part(start):
        part = slice(start * side, (start + count) * side)
        left = product(first[part], w11, COLS)
        rest.append(second[part] - product(left, r12, PLAIN))
        for line in range(count):
            basis[start + line, :, :TILE] = left[line * side : (line + 1) * side] * scale

    tasks = [functools.partial(early_part, start) for start in range(0, lines, count)]
    r22, w22 = solve(a22, tasks)
    right = product(jnp.concatenate(rest, axis=0), w22 * scale, COLS)
    merged[:TILE, :TILE] = r11 * (1.0 / scale)
    merged[:TILE, TILE:] = r12 * (1.0 / scale)
    merged[TILE:, :TILE] = jnp.zeros((TILE, TILE), jnp.float32)
    merged[TILE:, TILE:] = r22 * (1.0 / scale)
    for line in range(lines):
        part = slice(line * side, (line + 1) * side)
        basis[line, :, TILE:] = right[part]


def shifted(kernel, rows, start):
    flat = jnp.concatenate([kernel, jnp.zeros((1, TILE - kernel.shape[1]), jnp.float32)], axis=1)
    return pltpu.roll(jnp.broadcast_to(flat, (rows, TILE)), start, 1, stride=1, stride_axis=0)


def smoother(kernel, side):
    pair = 2 * side
    row = lax.broadcasted_iota(jnp.int32, (pair, TILE), 0)
    lane = lax.broadcasted_iota(jnp.int32, (pair, TILE), 1)
    total = jnp.zeros((pair, TILE), jnp.float32)
    for part in range(3):
        place = lane - part * pair
        inside = (place >= 0) & (place < pair) & ((place >= side) == (row >= side))
        total = jnp.where(inside, shifted(kernel, pair, part * side), total)
    return total[:, : 3 * pair]


def stacked(before, own, after, first, count):
    part = slice(first, first + count)
    return jnp.concatenate([lines[part, :] for lines in (before, own, after)], axis=0)


def turned(out, line, side, value):
    out[pl.ds(line, side, stride=out.shape[0] // side), :] = value


def ordered(first, kernel, side):
    pair = 2 * side
    plain = smoother(kernel[...], side)
    lead, middle, trail = (plain[:, at : at + pair] for at in (0, pair, 2 * pair))
    swapped = jnp.concatenate([trail, middle, lead], axis=1)
    return jnp.where(first == 1, swapped, plain)


def filtered(taps, field, padded, start):
    rows, cols, hours = padded.shape
    side = field.shape[1]
    count = taps.shape[1]
    lane = lax.broadcasted_iota(jnp.int32, (1, count), 1)
    full = taps[...] + jnp.where(lane == TH, 1.0, 0.0)
    full = jnp.concatenate([full, jnp.zeros((1, hours - count), jnp.float32)], axis=1)
    skew = pltpu.roll(jnp.broadcast_to(full, (TILE, hours)), 0, 1, stride=1, stride_axis=0)
    padded[:, side:, :] = jnp.zeros((rows, cols - side, hours), jnp.float32)
    padded[:, :side, :] = field[:, :, start : start + hours]
    return product(padded[...].reshape(rows * cols, hours), skew, COLS)


def early_kernel(joined, field, out, taps_out, lat_out, lon_out, padded):
    start = 0
    for part in (taps_out, lat_out, lon_out):
        part[...] = joined[:, start : start + part.shape[1]]
        start += part.shape[1]
    rows, side, _ = field.shape
    result = filtered(taps_out, field, padded, 0)
    for row in range(rows):
        at = row * padded.shape[1]
        turned(out, row, side, result[at : at + side])


def late_kernel(low, weights, taps, lat_kernel, lon_kernel, field, out, lat_band, lon_band, padded):
    rows, side, _ = field.shape
    result = filtered(taps, field, padded, TILE)
    for row in range(rows):
        at = row * padded.shape[1]
        out[row * side : (row + 1) * side, :] = result[at : at + side]
    lon_band[...] = ordered(low[1], lon_kernel, SH)
    lat_band[...] = ordered(low[0], lat_kernel, SH) * weights[...]


def smooth_kernel(side, band, near, own, far, out):
    pair = 2 * side
    for first in range(0, out.shape[0], pair):
        result = product(band[...], stacked(near, own, far, first, pair), PLAIN)
        for line in range(2):
            turned(out, first // side + line, side, result[line * side : (line + 1) * side])


def packed_corner(first, second):
    lane = lax.broadcasted_iota(jnp.int32, (PACK, TILE), 1)
    return jnp.where(lane < PACK, pltpu.roll(second[PACK:], PACK, 1), first[PACK:])


def mirrored(top, corner):
    row = lax.broadcasted_iota(jnp.int32, (TILE, TILE), 0)
    lane = lax.broadcasted_iota(jnp.int32, (TILE, TILE), 1)
    upper = jnp.concatenate([top, corner], axis=0)
    return jnp.where((row >= PACK) & (lane < PACK), upper.T, upper)


def last_kernel(side, lon_band, lat_band, *refs):
    parts, (out, gram) = (refs[:-2], refs[-2:])
    pair = 2 * side
    for first in range(0, out.shape[1], pair):
        line = first // side
        out[0, first : first + pair, :] = product(lon_band[...], stacked(*parts[:3], first, pair), PLAIN)
        result = product(lat_band[...], stacked(*parts[3:], first, pair), PLAIN)
        for at in range(2):
            turned(out.at[1], line + at, side, result[at * side : (at + 1) * side])
    early, late = (out[0], out[1])
    first = product(early, early, ROWS)
    cross = product(early, late, ROWS)
    second = product(late, late, ROWS)
    packed = packed_corner(first, second)
    for at, block in enumerate((first[:PACK], cross[:PACK], cross[PACK:], second[:PACK], packed)):
        gram[at * PACK : (at + 1) * PACK, :] = block


def called(kernel, name, shapes, spaces, scratch, *args):
    spaces = list(spaces) + [pltpu.VMEM] * (len(args) - len(spaces))
    return pl.pallas_call(
        kernel,
        out_shape=[jax.ShapeDtypeStruct(shape, jnp.float32) for shape in shapes],
        in_specs=[pl.BlockSpec(memory_space=space) for space in spaces],
        out_specs=[pl.BlockSpec(memory_space=pltpu.VMEM)] * len(shapes),
        scratch_shapes=scratch,
        compiler_params=pltpu.CompilerParams(vmem_limit_bytes=24 * 1024 * 1024),
        name=name,
    )(*args)


def around(value):
    peers = lax.axis_size(LON)
    near = lax.ppermute(value, "core", [(0, 1), (1, 0)])
    across = [(i, (i + 1) % peers) for i in range(1, peers, 2)]
    return near, lax.ppermute(value, LON, across + [(j, i) for i, j in across])


def partnered(value):
    return lax.ppermute(value, "yh", [(0, 1), (1, 0)])


def passed_on(value):
    spots, halves = (lax.axis_size("x"), lax.axis_size("yh"))
    near = partnered(value)
    up = [(x * halves, (x + 1) * halves) for x in range(spots - 1)]
    down = [((x + 1) * halves + 1, x * halves + 1) for x in range(spots - 1)]
    return near, lax.ppermute(near, LAT, up + down)


def straight(value):
    across = [(at, at + 1) for at in range(1, lax.axis_size(LAT) - 1, 2)]
    return partnered(value), lax.ppermute(value, LAT, across + [(j, i) for i, j in across])


def body(field, lat_kernel, lon_kernel, time_taps):
    rows_lat, rows_lon, length_in = field.shape
    steps_out = length_in - 2 * TH
    lat_place = lax.axis_index(LAT)
    total_lat = rows_lat * lax.axis_size(LAT)
    local = rows_lat * rows_lon
    cells = local * lax.axis_size(LAT) * lax.axis_size(LON)
    tall = -(-rows_lon // STEP) * STEP
    line = lax.broadcasted_iota(jnp.int32, (2 * rows_lat, 1), 0) % rows_lat
    globrow = (lat_place * rows_lat + line).astype(jnp.float32)
    latitude = jnp.pi * (globrow + 0.5) / total_lat - jnp.pi / 2
    weights = jnp.sqrt(jnp.cos(latitude))
    half = (local, TILE)
    low = jnp.stack([lax.axis_index("yh") == 0, lax.axis_index("core") == 0]).astype(jnp.int32)
    padded = [pltpu.VMEM((rows_lat, tall, 2 * TILE), jnp.float32)]
    first, taps_row, lat_row, lon_row = called(
        early_kernel,
        "early",
        [half, (1, 2 * TH + 1), (1, 2 * SH + 1), (1, 2 * SH + 1)],
        [],
        padded,
        jnp.concatenate([time_taps, lat_kernel, lon_kernel])[None],
        field,
    )
    second, lat_band, lon_band = called(
        late_kernel,
        "late",
        [half] + [(2 * SH, 6 * SH)] * 2,
        [pltpu.SMEM],
        padded,
        low,
        weights,
        taps_row,
        lat_row,
        lon_row,
        field,
    )
    smooth = functools.partial(smooth_kernel, SH)
    near, far = passed_on(first)
    beside, beyond = around(second)
    (second,) = called(smooth, "lon", [half], [], [], lon_band, beside, second, beyond)
    (first,) = called(smooth, "lat", [half], [], [], lat_band, near, first, far)
    near, far = straight(second)
    beside, beyond = around(first)
    matrix, local_gram = called(
        functools.partial(last_kernel, SH),
        "last",
        [(2,) + half, (5 * PACK, TILE)],
        [],
        [],
        lon_band,
        lat_band,
        beside,
        first,
        beyond,
        near,
        second,
        far,
    )
    gram = summed(local_gram)
    basis, merged = called(
        functools.partial(factor_kernel, cells),
        "factor",
        [(rows_lat, rows_lon, steps_out), (steps_out, steps_out)],
        [],
        [pltpu.VMEM((TILE, 2 * TILE), jnp.float32)],
        gram,
        matrix,
    )
    return (basis, merged)


def solution(mesh):
    fine = jax.sharding.Mesh(mesh.devices.reshape(4, 2, 2, 8, 2), ("x", "yh", "yl", "z", "core"))
    placed = (P(LAT, LON, None), P(), P(), P())
    return jax.shard_map(
        body, mesh=fine, in_specs=placed, out_specs=(P(LAT, LON, None), P()), check_vma=False
    )
```

```python
import functools

import jax
import jax.numpy as jnp
from jax import lax
from jax.experimental import pallas as pl
from jax.experimental.pallas import tpu as pltpu
from jax.sharding import PartitionSpec as P

TH = 64
SH = 20
LAT = ("x", "yh")
LON = ("yl", "z", "core")


PLANE = ("x", "yh", "yl", "core")


def shared(value, axes):
    peers = lax.axis_size(axes)
    copies = jnp.broadcast_to(value[None], (peers,) + value.shape)
    return lax.all_to_all(copies, axes, 0, 0)


def summed(value):
    peers = lax.axis_size(PLANE)
    pieces = lax.all_to_all(value.reshape(peers, 1, value.size // peers), PLANE, 0, 0)
    piece = shared(pieces.sum(axis=0), ("z",)).sum(axis=0)
    return shared(piece, PLANE).reshape(value.shape)


TILE = 128
STEP = 8
PACK = TILE // 2

def product(left, right, over):
    return lax.dot_general(
        left,
        right,
        (over, ((), ())),
        precision=lax.Precision.HIGHEST,
        preferred_element_type=jnp.float32,
    )


def wide(value):
    return jnp.broadcast_to(value, (STEP, TILE))


def eliminate(work, tasks=()):
    for top in range(0, TILE, STEP):
        for task in tasks[top // STEP : top // STEP + 1]:
            task()
        flat = [wide(work[top + i:top + i + 1, :TILE]) for i in range(STEP)]
        left = {(i, j): wide(flat[i][:, top + j:top + j + 1]) for j in range(STEP) for i in range(j + 1)}
        rows = [[wide(work[top + i:top + i + 1, s:s + TILE]) for s in (0, TILE)] for i in range(STEP)]
        root, upper = [], {}
        for j in range(STEP):
            root.append(lax.rsqrt(left[j, j]))
            for i in range(j + 1, STEP):
                upper[j, i] = left[j, i] * root[j]
            for i in range(j + 1, STEP):
                for n in range(i, STEP):
                    left[i, n] = left[i, n] - upper[j, i] * upper[j, n]
        for j in range(STEP):
            rows[j] = [value * root[j] for value in rows[j]]
            for i in range(j + 1, STEP):
                rows[i] = [value - upper[j, i] * done for value, done in zip(rows[i], rows[j])]
        for j in range(STEP):
            for half in range(2):
                work[top + j:top + j + 1, half * TILE:(half + 1) * TILE] = rows[j][half][:1, :]
        for below in range(top + STEP, TILE, STEP):
            parts = [work[below:below + STEP, s:s + TILE] for s in (0, TILE)]
            factors = [wide(parts[0][:, top + j:top + j + 1]) for j in range(STEP)]
            for j in range(STEP):
                factors[j] = factors[j] * root[j]
                for i in range(j + 1, STEP):
                    factors[i] = factors[i] - upper[j, i] * factors[j]
            for half in range(2):
                terms = [factors[j] * rows[j][half] for j in range(STEP)]
                while len(terms) > 1:
                    terms = [one + other for one, other in zip(terms[::2], terms[1::2])]
                parts[half] = parts[half] - terms[0]
            for half in range(2):
                work[below:below + STEP, half * TILE:(half + 1) * TILE] = parts[half]


ROWS = ((0,), (0,))
COLS = ((1,), (1,))
PLAIN = ((1,), (0,))


def factor_kernel(cells, gram, matrix, basis, merged, work):
    row = lax.broadcasted_iota(jnp.int32, (TILE, TILE), 0)
    col = lax.broadcasted_iota(jnp.int32, (TILE, TILE), 1)
    eye = jnp.where(row == col, 1.0, 0.0).astype(jnp.float32)
    scale = float(cells) ** 0.5

    def solve(block, tasks=()):
        work[:, :TILE] = block
        work[:, TILE:] = eye
        eliminate(work, tasks)
        upper = jnp.where(row <= col, work[:, :TILE], 0.0)
        lower = jnp.where(row >= col, work[:, TILE:], 0.0)
        return upper, lower

    blocks = [gram[at * PACK : (at + 1) * PACK, :] for at in range(5)]
    r11, w11 = solve(mirrored(blocks[0], blocks[4]))
    r12 = product(w11, jnp.concatenate(blocks[1:3], axis=0), PLAIN)
    a22 = mirrored(blocks[3], pltpu.roll(blocks[4], PACK, 1)) - product(r12, r12, ROWS)
    first, second = (matrix[0], matrix[1])
    lines, side, _ = basis.shape
    count = 4
    rest = []

    def early_part(start):
        part = slice(start * side, (start + count) * side)
        left = product(first[part], w11, COLS)
        rest.append(second[part] - product(left, r12, PLAIN))
        for line in range(count):
            basis[start + line, :, :TILE] = left[line * side : (line + 1) * side] * scale

    tasks = [functools.partial(early_part, start) for start in range(0, lines, count)]
    r22, w22 = solve(a22, tasks)
    right = product(jnp.concatenate(rest, axis=0), w22 * scale, COLS)
    merged[:TILE, :TILE] = r11 * (1.0 / scale)
    merged[:TILE, TILE:] = r12 * (1.0 / scale)
    merged[TILE:, :TILE] = jnp.zeros((TILE, TILE), jnp.float32)
    merged[TILE:, TILE:] = r22 * (1.0 / scale)
    for line in range(lines):
        part = slice(line * side, (line + 1) * side)
        basis[line, :, TILE:] = right[part]


def shifted(kernel, rows, start):
    flat = jnp.concatenate([kernel, jnp.zeros((1, TILE - kernel.shape[1]), jnp.float32)], axis=1)
    return pltpu.roll(jnp.broadcast_to(flat, (rows, TILE)), start, 1, stride=1, stride_axis=0)


def smoother(kernel, side):
    pair = 2 * side
    row = lax.broadcasted_iota(jnp.int32, (pair, TILE), 0)
    lane = lax.broadcasted_iota(jnp.int32, (pair, TILE), 1)
    total = jnp.zeros((pair, TILE), jnp.float32)
    for part in range(3):
        place = lane - part * pair
        inside = (place >= 0) & (place < pair) & ((place >= side) == (row >= side))
        total = jnp.where(inside, shifted(kernel, pair, part * side), total)
    return total[:, : 3 * pair]


def stacked(before, own, after, first, count):
    part = slice(first, first + count)
    return jnp.concatenate([lines[part, :] for lines in (before, own, after)], axis=0)


def turned(out, line, side, value):
    out[pl.ds(line, side, stride=out.shape[0] // side), :] = value


def ordered(first, kernel, side):
    pair = 2 * side
    plain = smoother(kernel[...], side)
    lead, middle, trail = (plain[:, at : at + pair] for at in (0, pair, 2 * pair))
    swapped = jnp.concatenate([trail, middle, lead], axis=1)
    return jnp.where(first == 1, swapped, plain)


def filtered(taps, field, padded, start):
    rows, cols, hours = padded.shape
    side = field.shape[1]
    count = taps.shape[1]
    lane = lax.broadcasted_iota(jnp.int32, (1, count), 1)
    full = taps[...] + jnp.where(lane == TH, 1.0, 0.0)
    full = jnp.concatenate([full, jnp.zeros((1, hours - count), jnp.float32)], axis=1)
    skew = pltpu.roll(jnp.broadcast_to(full, (TILE, hours)), 0, 1, stride=1, stride_axis=0)
    padded[:, side:, :] = jnp.zeros((rows, cols - side, hours), jnp.float32)
    padded[:, :side, :] = field[:, :, start : start + hours]
    return product(padded[...].reshape(rows * cols, hours), skew, COLS)


def early_kernel(taps, lat_kernel, lon_kernel, field, out, lat_out, lon_out, padded):
    lat_out[...] = lat_kernel[...]
    lon_out[...] = lon_kernel[...]
    rows, side, _ = field.shape
    result = filtered(taps, field, padded, 0)
    for row in range(rows):
        at = row * padded.shape[1]
        turned(out, row, side, result[at : at + side])


def late_kernel(low, weights, taps, lat_kernel, lon_kernel, field, out, lat_band, lon_band, padded):
    rows, side, _ = field.shape
    result = filtered(taps, field, padded, TILE)
    for row in range(rows):
        at = row * padded.shape[1]
        out[row * side : (row + 1) * side, :] = result[at : at + side]
    lon_band[...] = ordered(low[1], lon_kernel, SH)
    lat_band[...] = ordered(low[0], lat_kernel, SH) * weights[...]


def smooth_kernel(side, band, near, own, far, out):
    pair = 2 * side
    for first in range(0, out.shape[0], pair):
        result = product(band[...], stacked(near, own, far, first, pair), PLAIN)
        for line in range(2):
            turned(out, first // side + line, side, result[line * side : (line + 1) * side])


def packed_corner(first, second):
    lane = lax.broadcasted_iota(jnp.int32, (PACK, TILE), 1)
    return jnp.where(lane < PACK, pltpu.roll(second[PACK:], PACK, 1), first[PACK:])


def mirrored(top, corner):
    row = lax.broadcasted_iota(jnp.int32, (TILE, TILE), 0)
    lane = lax.broadcasted_iota(jnp.int32, (TILE, TILE), 1)
    upper = jnp.concatenate([top, corner], axis=0)
    return jnp.where((row >= PACK) & (lane < PACK), upper.T, upper)


def last_kernel(side, lon_band, lat_band, *refs):
    parts, (out, gram) = (refs[:-2], refs[-2:])
    pair = 2 * side
    for first in range(0, out.shape[1], pair):
        line = first // side
        out[0, first : first + pair, :] = product(lon_band[...], stacked(*parts[:3], first, pair), PLAIN)
        result = product(lat_band[...], stacked(*parts[3:], first, pair), PLAIN)
        for at in range(2):
            turned(out.at[1], line + at, side, result[at * side : (at + 1) * side])
    early, late = (out[0], out[1])
    first = product(early, early, ROWS)
    cross = product(early, late, ROWS)
    second = product(late, late, ROWS)
    packed = packed_corner(first, second)
    for at, block in enumerate((first[:PACK], cross[:PACK], cross[PACK:], second[:PACK], packed)):
        gram[at * PACK : (at + 1) * PACK, :] = block


def called(kernel, name, shapes, spaces, scratch, *args):
    spaces = list(spaces) + [pltpu.VMEM] * (len(args) - len(spaces))
    return pl.pallas_call(
        kernel,
        out_shape=[jax.ShapeDtypeStruct(shape, jnp.float32) for shape in shapes],
        in_specs=[pl.BlockSpec(memory_space=space) for space in spaces],
        out_specs=[pl.BlockSpec(memory_space=pltpu.VMEM)] * len(shapes),
        scratch_shapes=scratch,
        compiler_params=pltpu.CompilerParams(vmem_limit_bytes=24 * 1024 * 1024),
        name=name,
    )(*args)


def around(value):
    peers = lax.axis_size(LON)
    near = lax.ppermute(value, "core", [(0, 1), (1, 0)])
    across = [(i, (i + 1) % peers) for i in range(1, peers, 2)]
    return near, lax.ppermute(value, LON, across + [(j, i) for i, j in across])


def partnered(value):
    return lax.ppermute(value, "yh", [(0, 1), (1, 0)])


def passed_on(value):
    spots, halves = (lax.axis_size("x"), lax.axis_size("yh"))
    near = partnered(value)
    up = [(x * halves, (x + 1) * halves) for x in range(spots - 1)]
    down = [((x + 1) * halves + 1, x * halves + 1) for x in range(spots - 1)]
    return near, lax.ppermute(near, LAT, up + down)


def straight(value):
    across = [(at, at + 1) for at in range(1, lax.axis_size(LAT) - 1, 2)]
    return partnered(value), lax.ppermute(value, LAT, across + [(j, i) for i, j in across])


def body(field, lat_kernel, lon_kernel, time_taps):
    rows_lat, rows_lon, length_in = field.shape
    steps_out = length_in - 2 * TH
    lat_place = lax.axis_index(LAT)
    total_lat = rows_lat * lax.axis_size(LAT)
    local = rows_lat * rows_lon
    cells = local * lax.axis_size(LAT) * lax.axis_size(LON)
    tall = -(-rows_lon // STEP) * STEP
    line = lax.broadcasted_iota(jnp.int32, (2 * rows_lat, 1), 0) % rows_lat
    globrow = (lat_place * rows_lat + line).astype(jnp.float32)
    latitude = jnp.pi * (globrow + 0.5) / total_lat - jnp.pi / 2
    weights = jnp.sqrt(jnp.cos(latitude))
    half = (local, TILE)
    low = jnp.stack([lax.axis_index("yh") == 0, lax.axis_index("core") == 0]).astype(jnp.int32)
    padded = [pltpu.VMEM((rows_lat, tall, 2 * TILE), jnp.float32)]
    first, lat_row, lon_row = called(
        early_kernel,
        "early",
        [half, (1, 2 * SH + 1), (1, 2 * SH + 1)],
        [],
        padded,
        time_taps[None],
        lat_kernel[None],
        lon_kernel[None],
        field,
    )
    second, lat_band, lon_band = called(
        late_kernel,
        "late",
        [half] + [(2 * SH, 6 * SH)] * 2,
        [pltpu.SMEM],
        padded,
        low,
        weights,
        time_taps[None],
        lat_row,
        lon_row,
        field,
    )
    smooth = functools.partial(smooth_kernel, SH)
    near, far = straight(first)
    beside, beyond = around(second)
    (second,) = called(smooth, "lon", [half], [], [], lon_band, beside, second, beyond)
    (first,) = called(smooth, "lat", [half], [], [], lat_band, near, first, far)
    near, far = straight(second)
    beside, beyond = around(first)
    matrix, local_gram = called(
        functools.partial(last_kernel, SH),
        "last",
        [(2,) + half, (5 * PACK, TILE)],
        [],
        [],
        lon_band,
        lat_band,
        beside,
        first,
        beyond,
        near,
        second,
        far,
    )
    gram = summed(local_gram)
    basis, merged = called(
        functools.partial(factor_kernel, cells),
        "factor",
        [(rows_lat, rows_lon, steps_out), (steps_out, steps_out)],
        [],
        [pltpu.VMEM((TILE, 2 * TILE), jnp.float32)],
        gram,
        matrix,
    )
    return (basis, merged)


def solution(mesh):
    fine = jax.sharding.Mesh(mesh.devices.reshape(4, 2, 2, 8, 2), ("x", "yh", "yl", "z", "core"))
    placed = (P(LAT, LON, None), P(), P(), P())
    return jax.shard_map(
        body, mesh=fine, in_specs=placed, out_specs=(P(LAT, LON, None), P()), check_vma=False
    )
```
